256 devices in a mesh: slab: 32 (over z, y), coil: 8 (over x, core).
Axes of the slice: x: 4, y: 4, z: 8, core: 2. Of those that a mesh axis runs over, the one named last changes fastest.
Arguments:
- image_x: float32 [384, 384, 32], P('slab'), may hold values from -6 to 6
- residual: float32 [384, 384, 32], P('slab'), may hold values from -15 to 15
- direction: float32 [384, 384, 32], P('slab'), may hold values from -15 to 15
- sensitivity: bfloat16 [384, 384, 1024], P('slab', None, 'coil'), may hold values from -0.29882812 to 0.29882812
- interp: float32 [32, 32, 4, 64, 128], P('slab'), may hold values from -0.75 to 0.75
- slot_tile: int32 [32, 32, 4], P('slab'), may hold values from 0 to 71
- counts: int32 [32, 32, 4], P('slab'), may hold values from 0 to 128, as said below
Outputs:
- next_image: float32 [384, 384, 32], P('slab')
- next_residual: float32 [384, 384, 32], P('slab')
- next_direction: float32 [384, 384, 32], P('slab')
The draws below stay inside these ranges and needn't reach their ends.
Inputs may be any that keep to these rules, and one draw needn't show every extreme that they name: `counts`: 0 marks an empty slot; some block in every draw has all 128 samples live.
All inputs are finite; a program needn't handle non-finite values.
Results may differ from the reference program's by a relative error of at most 0.0003.
Values sent between devices are 32-bit elements; how exact they have to be, the bound alone decides.
No kernel may reach another device: no remote copies, remote signals or barrier semaphores. Data moves between devices by JAX's collectives and lax.ppermute only.
A program may use at most 128 MiB of HBM per device.

```python
import jax
import jax.numpy as jnp
from jax import lax

NX = 384
NY = 384
C = 32
NZ = 16
CAP = 4
SB = 128
TX = 16
TY = 4
TILES = 72
N_SLAB = 32


def ramp_profile():
    return 1.0 + 2.0 * jnp.arange(NX, dtype=jnp.float32) / (NX - 1)


def draw_residual(key, part):
    key = jax.random.fold_in(key, 11)
    values = jax.random.truncated_normal(key, -5.0, 5.0, (NX, NY, 2 * NZ), jnp.float32)
    return values * ramp_profile()[:, None, None]


def draw_direction(key, part):
    key = jax.random.fold_in(key, 12)
    values = jax.random.truncated_normal(key, -5.0, 5.0, (NX, NY, 2 * NZ), jnp.float32)
    return values * ramp_profile()[:, None, None]


def draw_counts(key, part):
    key = jax.random.fold_in(key, 13)
    key_live, key_size = jax.random.split(key)
    owners = jnp.arange(N_SLAB, dtype=jnp.int32)
    distance = jnp.abs(2 * owners - (N_SLAB - 1))
    threshold = N_SLAB - distance
    rolled = jax.random.randint(key_live, (N_SLAB, N_SLAB, CAP), 0, N_SLAB, dtype=jnp.int32)
    amounts = jax.random.randint(key_size, (N_SLAB, N_SLAB, CAP), 1, SB + 1, dtype=jnp.int32)
    filled = jnp.where(rolled < threshold[None, :, None], amounts, 0)
    filled = filled.at[:, N_SLAB // 2, 0].set(SB)
    return filled.astype(jnp.int32)


def set_ends(drawn, own_key, low, top_value):
    index_at = [jax.random.randint(jax.random.fold_in(own_key, axis), (), 0, length) for axis, length in enumerate(drawn.shape)]
    widest = drawn.shape.index(max(drawn.shape))
    next_to = index_at[:widest] + [(index_at[widest] + 1) % drawn.shape[widest]] + index_at[widest + 1:]
    return drawn.at[tuple(index_at)].set(low).at[tuple(next_to)].set(top_value)


def level_of(rng, shape, cuts, least, largest):
    def one(axis_at, blocks):
        steps = jax.random.uniform(jax.random.fold_in(jax.random.fold_in(rng, 6), axis_at), (blocks,), jnp.float32, least / len(cuts), largest / len(cuts))
        return jnp.repeat(jnp.exp(steps), shape[axis_at] // blocks).reshape((-1,) + (1,) * (len(shape) - axis_at - 1))

    gain = one(*cuts[0])
    for cut in cuts[1:]:
        gain = gain * one(*cut)
    return gain


def normal_values(key, extent, scale, limit, cuts=(), kind=jnp.bfloat16):
    entries = scale * jax.random.normal(key, extent, jnp.float32)
    if cuts:
        entries = entries * level_of(key, extent, cuts, -0.22, 0.18)
    return jnp.clip(entries, -limit, limit).astype(kind)


def setup_inputs(seed: int = 0) -> dict:
    streams_of = jax.random.split(jax.random.key(seed), 8)
    return {
        "image_x": normal_values(streams_of[0], (NX, NY, 2 * NZ), 1.0, 6.0, ((0, 32),), jnp.float32),
        "residual": draw_residual(jax.random.fold_in(streams_of[7], 71), 0),
        "direction": draw_direction(jax.random.fold_in(streams_of[7], 71), 0),
        "sensitivity": jnp.clip(jax.random.uniform(streams_of[3], (NX, NY, C * 2 * NZ), jnp.float32, -0.29882812, 0.29882812) * level_of(streams_of[3], (NX, NY, C * 2 * NZ), ((0, 32), (2, 8)), -0.4, 0.0), -0.29882812, 0.29882812).astype(jnp.bfloat16),
        "interp": normal_values(streams_of[4], (N_SLAB, N_SLAB, CAP, TX * TY, SB), (TX * TY) ** -0.5, 0.75, ((0, 32),), jnp.float32),
        "slot_tile": set_ends(jax.random.randint(streams_of[5], (N_SLAB, N_SLAB, CAP), 0, TILES), jax.random.fold_in(streams_of[5], 1), 0, TILES - 1).astype(jnp.int32),
        "counts": draw_counts(jax.random.fold_in(streams_of[7], 71), 0),
    }


def reference(image_x, residual, direction, sensitivity, interp, slot_tile, counts):
    ky_dev = NY // N_SLAB
    tiles_dev = (NX // TX) * (ky_dev // TY)
    cells = TX * TY
    dir_real = direction[:, :, :NZ]
    dir_imag = direction[:, :, NZ:]
    coil_maps = jnp.moveaxis(sensitivity.reshape(NX, NY, C, 2 * NZ), 2, 0)
    owner_weights = jnp.transpose(interp, (1, 0, 2, 3, 4))
    owner_counts = jnp.transpose(counts, (1, 0, 2))
    sample_ids = jnp.arange(SB, dtype=jnp.int32)
    live_mask = (sample_ids[None, None, None, :] < owner_counts[..., None]).astype(jnp.float32)
    flat_ids = (jnp.arange(N_SLAB, dtype=jnp.int32)[:, None, None] * tiles_dev + slot_tile).reshape(-1).astype(jnp.int32)

    def per_coil(running, one_map):
        maps = one_map.astype(jnp.float32)
        map_real = maps[:, :, :NZ]
        map_imag = maps[:, :, NZ:]
        weighted = (map_real * dir_real - map_imag * dir_imag) + 1j * (map_real * dir_imag + map_imag * dir_real)
        spectrum = jnp.fft.fft2(weighted, axes=(0, 1), norm="ortho")
        stacked = jnp.concatenate([spectrum.real, spectrum.imag], axis=2)
        tiles = stacked.reshape(NX // TX, TX, N_SLAB, ky_dev // TY, TY, 2 * NZ)
        tiles = jnp.transpose(tiles, (2, 0, 3, 1, 4, 5)).reshape(N_SLAB * tiles_dev, cells, 2 * NZ)
        picked = tiles[flat_ids].reshape(N_SLAB, N_SLAB, CAP, cells, 2 * NZ)
        samples = jnp.einsum('orjcs,orjcq->orjsq', owner_weights, picked, precision=lax.Precision.HIGHEST)
        samples = samples * live_mask[..., None]
        spread = jnp.einsum('orjcs,orjsq->orjcq', owner_weights, samples, precision=lax.Precision.HIGHEST)
        summed = jax.ops.segment_sum(spread.reshape(-1, cells, 2 * NZ), flat_ids, num_segments=N_SLAB * tiles_dev)
        grid_cells = summed.reshape(N_SLAB, NX // TX, ky_dev // TY, TX, TY, 2 * NZ)
        grid_cells = jnp.transpose(grid_cells, (1, 3, 0, 2, 4, 5)).reshape(NX, NY, 2 * NZ)
        complex_grid = grid_cells[:, :, :NZ] + 1j * grid_cells[:, :, NZ:]
        coil_back = jnp.fft.ifft2(complex_grid, axes=(0, 1), norm="ortho")
        real_part = map_real * coil_back.real + map_imag * coil_back.imag
        imag_part = map_real * coil_back.imag - map_imag * coil_back.real
        return running + jnp.concatenate([real_part, imag_part], axis=2), None

    applied, _ = lax.scan(per_coil, jnp.zeros((NX, NY, 2 * NZ), jnp.float32), coil_maps)
    norm_now = jnp.sum(residual * residual)
    curvature = jnp.sum(direction * applied)
    step_size = norm_now / curvature
    next_image = image_x + step_size * direction
    next_residual = residual - step_size * applied
    norm_next = jnp.sum(next_residual * next_residual)
    next_direction = next_residual + (norm_next / norm_now) * direction
    return next_image, next_residual, next_direction
```

```python
import jax
import jax.numpy as jnp
import ml_dtypes
import numpy as np
from jax import lax
from jax.experimental import pallas as pl
from jax.experimental.pallas import tpu as pltpu
from jax.sharding import Mesh
from jax.sharding import PartitionSpec as P

N = 384
SLABS = 32
ROWS = 12
PAIRS = ROWS // 2
LANES = 128
PLANES = 16
TX = 16
TY = 4
CELLS = TX * TY
TILES = 72
CAP = 4
SB = 128
SLAB = ("z", "y")
COIL = ("x", "core")
ALL = ("z", "y", "x", "core")
VMEM_LIMIT = 56 * 1024 * 1024
F32 = jnp.float32
BF16 = jnp.bfloat16
NT = (((1,), (1,)), ((), ()))


def split_table(table):
    table = table.astype(np.float32)
    high = table.astype(ml_dtypes.bfloat16)
    low = (table - high.astype(np.float32)).astype(ml_dtypes.bfloat16)
    return high, low


def dft_tables():
    pos = np.arange(N)
    phase = (pos[:, None] * pos[None, :] % N) * (2.0 * np.pi / N)
    real = np.cos(phase) / np.sqrt(N)
    imag = -np.sin(phase) / np.sqrt(N)
    base = ROWS * np.arange(SLABS)[:, None]
    rows = np.concatenate([(base + np.arange(8)).reshape(-1), (base + np.arange(8, ROWS)).reshape(-1)])
    cols = np.concatenate([(base + 2 * np.arange(PAIRS) + i).reshape(-1) for i in range(2)])
    return split_table(np.concatenate([real[rows], imag[rows]])), split_table(np.concatenate([real[:, cols], imag[:, cols]]))


def split(value):
    high = value.astype(BF16)
    return high, (value - high.astype(F32)).astype(BF16)


def dot(a, b):
    return jnp.dot(a, b, preferred_element_type=F32)


def dot3(a_high, a_low, b_high, b_low):
    return dot(a_high, b_high) + (dot(a_high, b_low) + dot(a_low, b_high))


def dot_nt(a, b):
    return lax.dot_general(a, b, NT, preferred_element_type=F32)


def imag_lanes(shape):
    return lax.broadcasted_iota(jnp.int32, shape, 1) // PLANES % 2 == 1


def times_i(value, imag):
    lanes = value.shape[1]
    return jnp.where(imag, pltpu.roll(value, PLANES, 1), -pltpu.roll(value, lanes - PLANES, 1))


def spread_maps(maps, imag):
    real_part = jnp.where(imag, pltpu.roll(maps, PLANES, 1), maps)
    imag_part = jnp.where(imag, maps, pltpu.roll(maps, LANES - PLANES, 1))
    return real_part, imag_part


def store_outgoing(out_ref, start, even, odd):
    out_ref[:, start:start + 8, :] = even[:256].reshape(SLABS, 8, LANES)
    out_ref[:, start + 8:start + 16, :] = odd[:256].reshape(SLABS, 8, LANES)
    lower = lax.broadcasted_iota(jnp.int32, (8, LANES), 0) < 4
    for m in range(SLABS // 2):
        first = even[256 + 8 * m:264 + 8 * m]
        second = odd[256 + 8 * m:264 + 8 * m]
        out_ref[2 * m, start + 16:start + 24, :] = jnp.where(lower, first, pltpu.roll(second, 4, 0))
        out_ref[2 * m + 1, start + 16:start + 24, :] = jnp.where(lower, pltpu.roll(first, 4, 0), second)


def arrived_rows(ref, index):
    parts = []
    for i in range(2):
        start = i * 8 + index if index < 8 else 16 + 4 * i + index - 8
        parts.append(ref[pl.ds(start, SLABS * PAIRS, stride=24), :])
    return jnp.concatenate(parts, axis=0)


def gram_kernel(coil_ref, counts_ref, w_ref, out_ref, scratch):
    step = pl.program_id(0)
    owners = w_ref.shape[0]
    coil = coil_ref[0]
    lane = lax.broadcasted_iota(jnp.int32, (8, SB), 1)
    for o in range(owners):
        for j in range(CAP):
            for v in range(TY):
                at = (j * TY + v) * TX
                scratch[o % 2, at:at + TX, :] = w_ref[o, j, pl.ds(v, TX, stride=TY), :]
        rows = []
        for j in range(CAP):
            mine = scratch[o % 2, pl.ds(pl.multiple_of(j * CELLS + coil * 8, 8), 8), :]
            live = counts_ref[(step * owners + o) * CAP + j]
            rows.append(jnp.where(lane < live, mine, 0.0))
        l_high, l_low = split(jnp.concatenate(rows, axis=0))
        r_high, r_low = split(scratch[o % 2])
        gram = dot_nt(l_high, r_high) + (dot_nt(l_high, r_low) + dot_nt(l_low, r_high))
        for m in range(CAP // 2):
            first = gram[16 * m:16 * m + 8, LANES * m:LANES * (m + 1)]
            second = gram[16 * m + 8:16 * m + 16, LANES * m:LANES * (m + 1)]
            out_ref[o, 8 * m:8 * m + 8, :] = jnp.where(lane < CELLS, first, second)


def gram_rows(interp, counts, coil):
    owners = 4
    return pl.pallas_call(
        gram_kernel,
        grid=(SLABS // owners,),
        in_specs=[
            pl.BlockSpec(memory_space=pltpu.SMEM),
            pl.BlockSpec(memory_space=pltpu.SMEM),
            pl.BlockSpec((owners, CAP, CELLS, SB), lambda i: (i, 0, 0, 0)),
        ],
        out_specs=pl.BlockSpec((owners, 16, LANES), lambda i: (i, 0, 0)),
        out_shape=jax.ShapeDtypeStruct((SLABS, 16, LANES), F32),
        scratch_shapes=[pltpu.VMEM((2, CAP * CELLS, SB), F32)],
        compiler_params=pltpu.CompilerParams(vmem_limit_bytes=VMEM_LIMIT),
        name="gram_rows",
    )(coil, counts, interp)


def gram_sum_kernel(tiles_ref, in_ref, out_ref, total):
    total[...] = jnp.zeros_like(total)
    lane = lax.broadcasted_iota(jnp.int32, (8, LANES), 1)

    def add(r, carry):
        for j in range(CAP):
            tile = tiles_ref[r * CAP + j]
            piece = in_ref[r, 8 * (j // 2):8 * (j // 2) + 8, :]
            keep = lane < CELLS if j % 2 == 0 else lane >= CELLS
            total[tile] = total[tile] + jnp.where(keep, piece, 0.0)
        return carry

    lax.fori_loop(0, SLABS, add, 0)
    groups = N // TX // 2
    for b in range(ROWS // TY):
        for m in range(groups):
            first = total[2 * m * 3 + b]
            second = total[(2 * m + 1) * 3 + b]
            first = first + pltpu.roll(first, CELLS, 1)
            second = second + pltpu.roll(second, CELLS, 1)
            at = (b * groups + m) * 8
            out_ref[at:at + 8, :] = jnp.where(lane < CELLS, first, second)


def gram_sum(arrived, tiles):
    return pl.pallas_call(
        gram_sum_kernel,
        in_specs=[pl.BlockSpec(memory_space=pltpu.SMEM), pl.BlockSpec(memory_space=pltpu.VMEM)],
        out_specs=pl.BlockSpec(memory_space=pltpu.VMEM),
        out_shape=jax.ShapeDtypeStruct((TILES // 2 * 8, LANES), F32),
        scratch_shapes=[pltpu.VMEM((TILES, 8, LANES), F32)],
        compiler_params=pltpu.CompilerParams(vmem_limit_bytes=VMEM_LIMIT),
        name="gram_sum",
    )(tiles, arrived)


def forward_y_kernel(d_ref, s_ref, th_ref, tl_ref, out_ref):
    imag = imag_lanes((N, LANES))
    images = []
    for i in range(2):
        d = d_ref[i]
        wide = jnp.concatenate([d] * (LANES // (2 * PLANES)), axis=0).T
        real_map, imag_map = spread_maps(s_ref[i].astype(F32), imag)
        images.append(real_map * wide + imag_map * times_i(wide, imag))
    x_high, x_low = split(jnp.concatenate(images, axis=1))
    both = dot3(th_ref[...], tl_ref[...], x_high, x_low)
    done = []
    for i in range(2):
        half = both[:, LANES * i:LANES * (i + 1)]
        done.append(half[:N] + times_i(half[N:], imag))
    store_outgoing(out_ref, 0, done[0], done[1])


def forward_y(direction, maps, table):
    return pl.pallas_call(
        forward_y_kernel,
        grid=(PAIRS,),
        in_specs=[
            pl.BlockSpec((2, 2 * PLANES, N), lambda i: (i, 0, 0)),
            pl.BlockSpec((2, N, LANES), lambda i: (i, 0, 0)),
            pl.BlockSpec((2 * N, N), lambda i: (0, 0)),
            pl.BlockSpec((2 * N, N), lambda i: (0, 0)),
        ],
        out_specs=pl.BlockSpec((SLABS, 24, LANES), lambda i: (0, i, 0)),
        out_shape=jax.ShapeDtypeStruct((SLABS, 24 * PAIRS, LANES), F32),
        compiler_params=pltpu.CompilerParams(vmem_limit_bytes=VMEM_LIMIT),
        name="forward_y",
    )(direction, maps, *table)


def middle_kernel(in_ref, g_ref, fh_ref, fl_ref, bh_ref, bl_ref, out_ref, curve_ref, grid_ref):
    imag = imag_lanes((N, LANES))
    for p in range(PAIRS):
        x = jnp.concatenate([arrived_rows(in_ref, 2 * p), arrived_rows(in_ref, 2 * p + 1)], axis=1)
        x_high, x_low = split(x)
        both = dot3(fh_ref[...], fl_ref[...], x_high, x_low)
        for i in range(2):
            half = both[:, LANES * i:LANES * (i + 1)]
            grid_ref[2 * p + i] = half[:N] + times_i(half[N:], imag)
    left = lax.broadcasted_iota(jnp.int32, (CELLS, LANES), 1) < CELLS
    curve = jnp.zeros((8, LANES), F32)
    groups = N // TX // 2
    for b in range(ROWS // TY):
        for m in range(groups):
            at = (b * groups + m) * 8
            packed = jnp.concatenate([g_ref[c, at:at + 8, :] for c in range(8)], axis=0)
            weights = jnp.concatenate([jnp.where(left, packed, 0.0), jnp.where(left, 0.0, packed)], axis=0)
            tile = jnp.concatenate(
                [grid_ref[b * TY + v, (2 * m + h) * TX:(2 * m + h + 1) * TX, :] for h in range(2) for v in range(TY)],
                axis=0,
            )
            applied = dot3(*split(weights), *split(tile))
            product = tile * applied
            curve = curve + jnp.sum(product.reshape(2 * CELLS // 8, 8, LANES), axis=0)
            for h in range(2):
                for v in range(TY):
                    grid_ref[b * TY + v, (2 * m + h) * TX:(2 * m + h + 1) * TX, :] = applied[
                        h * CELLS + v * TX:h * CELLS + (v + 1) * TX
                    ]
    curve_ref[...] = curve
    for p in range(PAIRS):
        x_high, x_low = split(jnp.concatenate([grid_ref[2 * p], grid_ref[2 * p + 1]], axis=1))
        both = dot3(bh_ref[...], bl_ref[...], x_high, x_low)
        done = []
        for i in range(2):
            half = both[:, LANES * i:LANES * (i + 1)]
            done.append(half[:N] - times_i(half[N:], imag))
        store_outgoing(out_ref, 24 * p, done[0], done[1])


def middle(arrived, grams, table_in, table_out):
    vmem = pl.BlockSpec(memory_space=pltpu.VMEM)
    return pl.pallas_call(
        middle_kernel,
        in_specs=[vmem] * 6,
        out_specs=[vmem, vmem],
        out_shape=[
            jax.ShapeDtypeStruct((SLABS, 24 * PAIRS, LANES), F32),
            jax.ShapeDtypeStruct((8, LANES), F32),
        ],
        scratch_shapes=[pltpu.VMEM((ROWS, N, LANES), F32)],
        compiler_params=pltpu.CompilerParams(vmem_limit_bytes=VMEM_LIMIT),
        name="middle",
    )(arrived, grams, *table_in, *table_out)


def backward_y_kernel(in_ref, s_ref, th_ref, tl_ref, out_ref):
    imag = imag_lanes((N, LANES))
    adder = (
        lax.broadcasted_iota(jnp.int32, (2 * PLANES, LANES), 1) % (2 * PLANES)
        == lax.broadcasted_iota(jnp.int32, (2 * PLANES, LANES), 0)
    ).astype(BF16)
    for p in range(PAIRS):
        x = jnp.concatenate([arrived_rows(in_ref, 2 * p), arrived_rows(in_ref, 2 * p + 1)], axis=1)
        x_high, x_low = split(x)
        both = dot3(th_ref[...], tl_ref[...], x_high, x_low)
        for i in range(2):
            half = both[:, LANES * i:LANES * (i + 1)]
            back = half[:N] - times_i(half[N:], imag)
            real_map, imag_map = spread_maps(s_ref[2 * p + i].astype(F32), imag)
            high, low = split(real_map * back - imag_map * times_i(back, imag))
            out_ref[2 * p + i] = dot_nt(adder, high) + dot_nt(adder, low)


def backward_y(arrived, maps, table):
    vmem = pl.BlockSpec(memory_space=pltpu.VMEM)
    return pl.pallas_call(
        backward_y_kernel,
        in_specs=[vmem] * 4,
        out_specs=vmem,
        out_shape=jax.ShapeDtypeStruct((ROWS, 2 * PLANES, N), F32),
        compiler_params=pltpu.CompilerParams(vmem_limit_bytes=VMEM_LIMIT),
        name="backward_y",
    )(arrived, maps, *table)


def all_sum(value, axis, count):
    step = 1
    while step < count:
        value = value + lax.ppermute(value, axis, [(i, i ^ step) for i in range(count)])
        step *= 2
    return value


def body(image_x, residual, direction, sensitivity, interp, slot_tile, counts):
    rows_table, cols_table = dft_tables()
    rows_table = tuple(jnp.asarray(t) for t in rows_table)
    cols_table = tuple(jnp.asarray(t) for t in cols_table)
    image_t, residual_t, direction_t = (jnp.transpose(a, (0, 2, 1)) for a in (image_x, residual, direction))
    coil = lax.axis_index(COIL).astype(jnp.int32)
    core = lax.axis_index("core")
    xpos = lax.axis_index("x")

    grams = gram_rows(interp[0], counts[0].reshape(-1), coil.reshape(1))
    grams = lax.all_to_all(grams, SLAB, split_axis=0, concat_axis=0, tiled=True)
    grams = gram_sum(grams, slot_tile[0].reshape(-1))
    grams = lax.all_gather(grams, COIL, axis=0, tiled=False)

    outgoing = forward_y(direction_t, sensitivity, rows_table)
    pencils = lax.all_to_all(outgoing, SLAB, split_axis=0, concat_axis=0, tiled=True)
    outgoing, curve = middle(pencils.reshape(-1, LANES), grams, cols_table, rows_table)
    norms = jnp.stack([jnp.sum(curve), 0.125 * jnp.sum(residual * residual)])
    norms = jnp.broadcast_to(norms[:, None, None], (2, 4, LANES)).reshape(8, LANES)
    norms = all_sum(all_sum(norms, COIL, 8), SLAB, SLABS)
    slab_rows = lax.all_to_all(outgoing, SLAB, split_axis=0, concat_axis=0, tiled=True)
    local = backward_y(slab_rows.reshape(-1, LANES), sensitivity, cols_table)

    curvature = norms[0, 0]
    norm_now = norms[4, 0]
    step_size = norm_now / curvature
    halves = local.reshape(2, N // 2, N)
    kept = lax.dynamic_index_in_dim(halves, core, 0, keepdims=False)
    sent = lax.dynamic_index_in_dim(halves, 1 - core, 0, keepdims=False)
    kept = kept + lax.ppermute(sent, "core", [(0, 1), (1, 0)])
    shares = lax.all_to_all(kept.reshape(4, N // 8, N), "x", split_axis=0, concat_axis=0, tiled=True)
    applied = jnp.sum(shares, axis=0)
    own = lax.dynamic_slice_in_dim(residual_t.reshape(N, N), core * (N // 2) + xpos * (N // 8), N // 8, 0)
    own = own - step_size * applied
    norm_next = jnp.broadcast_to(jnp.sum(own * own), (256, 1, LANES))
    norm_next = jnp.sum(lax.all_to_all(norm_next, ALL, split_axis=0, concat_axis=0, tiled=True)[:, 0, 0])
    other = lax.ppermute(own, "core", [(0, 1), (1, 0)])
    both = jnp.where(core == 0, jnp.stack([own, other]), jnp.stack([other, own]))
    full = jnp.zeros((2, 4, N // 8, N), F32)
    full = lax.dynamic_update_slice(full, both[:, None], (0, xpos, 0, 0))
    for d in range(1, 4):
        got = lax.ppermute(both, "x", [(i, (i + d) % 4) for i in range(4)])
        full = lax.dynamic_update_slice(full, got[:, None], (0, (xpos + 4 - d) % 4, 0, 0))
    next_residual = full.reshape(ROWS, 2 * PLANES, N)
    next_image = image_t + step_size * direction_t
    next_direction = next_residual + norm_next / norm_now * direction_t
    return tuple(jnp.transpose(a, (0, 2, 1)) for a in (next_image, next_residual, next_direction))


def solution(mesh):
    fine = Mesh(mesh.devices.reshape(8, 4, 4, 2), ALL)
    rows = P(SLAB, None, None)
    return jax.shard_map(
        body,
        mesh=fine,
        in_specs=(
            rows,
            rows,
            rows,
            P(SLAB, None, COIL),
            P(SLAB, None, None, None, None),
            rows,
            rows,
        ),
        out_specs=(rows, rows, rows),
        check_vma=False,
    )
```

```python
import jax
import jax.numpy as jnp
import ml_dtypes
import numpy as np
from jax import lax
from jax.experimental import pallas as pl
from jax.experimental.pallas import tpu as pltpu
from jax.sharding import Mesh
from jax.sharding import PartitionSpec as P

N = 384
SLABS = 32
ROWS = 12
PAIRS = ROWS // 2
LANES = 128
PLANES = 16
TX = 16
TY = 4
CELLS = TX * TY
TILES = 72
CAP = 4
SB = 128
SLAB = ("z", "y")
COIL = ("x", "core")
ALL = ("z", "y", "x", "core")
HALF_ROWS = PAIRS * 2 * PLANES
BLOCK = 24 * PAIRS
HALF = LANES // 2
COILS = HALF // PLANES
VMEM_LIMIT = 56 * 1024 * 1024
F32 = jnp.float32
BF16 = jnp.bfloat16
NT = (((1,), (1,)), ((), ()))


def split_table(table):
    table = table.astype(np.float32)
    high = table.astype(ml_dtypes.bfloat16)
    low = (table - high.astype(np.float32)).astype(ml_dtypes.bfloat16)
    return high, low


def dft_tables():
    pos = np.arange(N)
    phase = (pos[:, None] * pos[None, :] % N) * (2.0 * np.pi / N)
    real = np.cos(phase) / np.sqrt(N)
    imag = -np.sin(phase) / np.sqrt(N)
    base = ROWS * np.arange(SLABS)[:, None]
    rows = np.concatenate([(base + np.arange(8)).reshape(-1), (base + np.arange(8, ROWS)).reshape(-1)])
    cols = np.concatenate([base.reshape(-1) + 2 * p + i for i in range(2) for p in range(PAIRS)])
    sending = [split_table(np.concatenate([real[rows], sign * imag[rows]], axis=1)) for sign in (1, -1)]
    arrival = [split_table(np.concatenate([real[:, cols], sign * imag[:, cols]], axis=1)) for sign in (1, -1)]
    return sending, arrival


def selections():
    place = np.arange(LANES)
    part, coil, plane = place // HALF, place // PLANES % COILS, place % PLANES
    group, src_part, src_plane = place // (2 * PLANES), place // PLANES % 2, place % PLANES
    same = (group[:, None] == coil) & (src_plane[:, None] == plane)
    maps = np.concatenate([same & (src_part[:, None] == 0), same & (src_part[:, None] == 1)], axis=1)
    spread, gather = [], []
    for r in range(4):
        hit = (group[:, None] == r) & (src_plane[:, None] == plane)
        from_real = hit & (src_part[:, None] == 0)
        from_imag = hit & (src_part[:, None] == 1)
        spread.append((from_real & (part == 0)) + (from_imag & (part == 1)) + 0.0)
        spread.append((from_real & (part == 1)) + 0.0 - (from_imag & (part == 0)))
        gather.append((group == r) & (src_plane == plane[:, None]) & (src_part == part[:, None]))
    spread = np.concatenate([np.concatenate(spread, axis=1)] * 2, axis=0)
    gather = np.concatenate(gather * 2, axis=0)
    return tuple(a.astype(ml_dtypes.bfloat16) for a in (maps, spread, gather))


def split(value):
    high = value.astype(BF16)
    return high, (value - high.astype(F32)).astype(BF16)


def dot(a, b):
    return jnp.dot(a, b, preferred_element_type=F32)


def dot_nt(a, b):
    return lax.dot_general(a, b, NT, preferred_element_type=F32)


def whole(array):
    return pl.BlockSpec(array.shape, lambda i: (0,) * array.ndim)


def times_i(value):
    rolled = pltpu.roll(value, HALF, 1)
    return jnp.where(lax.broadcasted_iota(jnp.int32, value.shape, 1) < HALF, -rolled, rolled)


def transform(high_ref, low_ref, pieces, turned):
    highs, lows = [], []
    for piece, turn in zip(pieces, turned):
        piece_high, piece_low = split(piece)
        turn_high, turn_low = split(turn)
        highs.append(jnp.concatenate([piece_high, turn_high], axis=0))
        lows.append(jnp.concatenate([piece_low, turn_low], axis=0))
    high = jnp.concatenate(highs, axis=1)
    low = jnp.concatenate(lows, axis=1)
    return dot(high_ref[...], high) + (dot(high_ref[...], low) + dot(low_ref[...], high))


def store_outgoing(out_ref, start, even, odd):
    out_ref[:, start:start + 8, :] = even[:256].reshape(SLABS, 8, LANES)
    out_ref[:, start + 8:start + 16, :] = odd[:256].reshape(SLABS, 8, LANES)
    lower = lax.broadcasted_iota(jnp.int32, (8, LANES), 0) < 4
    for m in range(SLABS // 2):
        first = even[256 + 8 * m:264 + 8 * m]
        second = odd[256 + 8 * m:264 + 8 * m]
        out_ref[2 * m, start + 16:start + 24, :] = jnp.where(lower, first, pltpu.roll(second, 4, 0))
        out_ref[2 * m + 1, start + 16:start + 24, :] = jnp.where(lower, pltpu.roll(first, 4, 0), second)


def gram_sum_kernel(tiles_ref, in_ref, out_ref, total):
    total[...] = jnp.zeros_like(total)
    lane = lax.broadcasted_iota(jnp.int32, (8, LANES), 1)

    def add(r, carry):
        for j in range(CAP):
            tile = tiles_ref[j, r]
            piece = in_ref[r, 8 * (j // 2):8 * (j // 2) + 8, :]
            keep = lane < CELLS if j % 2 == 0 else lane >= CELLS
            total[tile] = total[tile] + jnp.where(keep, piece, 0.0)
        return carry

    lax.fori_loop(0, SLABS, add, 0)
    groups = N // TX // 2
    for b in range(ROWS // TY):
        for m in range(groups):
            first = total[2 * m * 3 + b]
            second = total[(2 * m + 1) * 3 + b]
            first = first + pltpu.roll(first, CELLS, 1)
            second = second + pltpu.roll(second, CELLS, 1)
            at = (b * groups + m) * 8
            out_ref[at:at + 8, :] = jnp.where(lane < CELLS, first, second)


def gram_sum(arrived, tiles):
    return pl.pallas_call(
        gram_sum_kernel,
        in_specs=[pl.BlockSpec(memory_space=pltpu.SMEM), pl.BlockSpec(memory_space=pltpu.VMEM)],
        out_specs=pl.BlockSpec(memory_space=pltpu.VMEM),
        out_shape=jax.ShapeDtypeStruct((TILES // 2 * 8, LANES), F32),
        scratch_shapes=[pltpu.VMEM((TILES, 8, LANES), F32)],
        compiler_params=pltpu.CompilerParams(vmem_limit_bytes=VMEM_LIMIT),
        name="gram_sum",
    )(tiles, arrived)


def forward_y_kernel(d_ref, s_ref, maps_ref, spread_ref, high_ref, low_ref, out_ref):
    flipped = d_ref[...].reshape(LANES, N).T
    wide = dot(jnp.concatenate(split(flipped), axis=1), spread_ref[...])
    for p in range(2):
        images, turned = [], []
        for r in (2 * p, 2 * p + 1):
            maps = dot(s_ref[r], maps_ref[...])
            real_map, imag_map = maps[:, :LANES], maps[:, LANES:]
            d = wide[:, 2 * r * LANES:(2 * r + 1) * LANES]
            turned_d = wide[:, (2 * r + 1) * LANES:(2 * r + 2) * LANES]
            images.append(real_map * d + imag_map * turned_d)
            turned.append(real_map * turned_d - imag_map * d)
        done = transform(high_ref, low_ref, images, turned)
        store_outgoing(out_ref, 24 * p, done[:, :LANES], done[:, LANES:])


def forward_y(direction, maps, sel_maps, sel_spread, table):
    return pl.pallas_call(
        forward_y_kernel,
        grid=(ROWS // 4,),
        in_specs=[
            pl.BlockSpec((4, 2 * PLANES, N), lambda i: (i, 0, 0)),
            pl.BlockSpec((4, N, LANES), lambda i: (i, 0, 0)),
            whole(sel_maps),
            whole(sel_spread),
            whole(table[0]),
            whole(table[1]),
        ],
        out_specs=pl.BlockSpec((SLABS, 48, LANES), lambda i: (0, i, 0)),
        out_shape=jax.ShapeDtypeStruct((SLABS, 24 * PAIRS, LANES), F32),
        compiler_params=pltpu.CompilerParams(vmem_limit_bytes=VMEM_LIMIT),
        name="forward_y",
    )(direction, maps, sel_maps, sel_spread, *table)


def arrived_rows(ref, index, block):
    parts = []
    for i in range(2):
        start = i * 8 + index if index < 8 else 16 + 4 * i + index - 8
        parts += [ref[pl.ds(start + 24 * p, SLABS, stride=block), :] for p in range(PAIRS)]
    return jnp.concatenate(parts, axis=0)


def middle_kernel(norm_ref, in_ref, *rest):
    g_refs = rest[:8]
    fh_ref, fl_ref, bh_ref, bl_ref, out_ref, grid_ref, g_ref = rest[8:]
    xpos, core = lax.axis_index("x"), lax.axis_index("core")
    for d in range(4):
        x = lax.rem(xpos + 4 - d, 4)
        for k in range(2):
            g_ref[2 * x + lax.rem(core + k, 2)] = g_refs[4 * k + d][...]
    for p in range(PAIRS):
        pieces = [arrived_rows(in_ref, 2 * p + i, BLOCK) for i in range(2)]
        done = transform(fh_ref, fl_ref, pieces, [times_i(x) for x in pieces])
        for i in range(2):
            b = 2 * p + i
            grid_ref[b // TY, pl.ds(b % TY, N, stride=TY), :] = done[:, LANES * i:LANES * (i + 1)]
    left = lax.broadcasted_iota(jnp.int32, (CELLS, LANES), 1) < CELLS
    curve = jnp.zeros((8, LANES), F32)
    groups = N // TX // 2
    for b in range(ROWS // TY):
        for m in range(groups):
            at = (b * groups + m) * 8
            packed = jnp.concatenate([g_ref[c, at:at + 8, :] for c in range(8)], axis=0)
            weights = jnp.concatenate([jnp.where(left, packed, 0.0), jnp.where(left, 0.0, packed)], axis=0)
            cells = slice(2 * m * CELLS, (2 * m + 2) * CELLS)
            tile = grid_ref[b, cells, :]
            w_high, w_low = split(weights)
            t_high, t_low = split(tile)
            applied = dot(jnp.concatenate([w_high, w_low], axis=1), jnp.concatenate([t_high, t_high], axis=0))
            applied = applied + dot(w_high, t_low)
            curve = curve + jnp.sum((tile * applied).reshape(2 * CELLS // 8, 8, LANES), axis=0)
            grid_ref[b, cells, :] = applied
    norm = jnp.broadcast_to(norm_ref[...], (8, LANES)) / (8 * LANES)
    sums = jnp.where(lax.broadcasted_iota(jnp.int32, (8, LANES), 0) == 0, jnp.sum(curve, axis=0, keepdims=True), norm)
    out_ref[:, BLOCK:, :] = jnp.broadcast_to(sums[None], (SLABS, 8, LANES))
    for p in range(PAIRS):
        pieces = [grid_ref[b // TY, pl.ds(b % TY, N, stride=TY), :] for b in (2 * p, 2 * p + 1)]
        done = transform(bh_ref, bl_ref, pieces, [times_i(x) for x in pieces])
        store_outgoing(out_ref, 24 * p, done[:, :LANES], done[:, LANES:])


def middle(norm, arrived, grams, table_in, table_out):
    vmem = pl.BlockSpec(memory_space=pltpu.VMEM)
    return pl.pallas_call(
        middle_kernel,
        in_specs=[vmem] * 14,
        out_specs=vmem,
        out_shape=jax.ShapeDtypeStruct((SLABS, BLOCK + 8, LANES), F32),
        scratch_shapes=[
            pltpu.VMEM((ROWS // TY, N * TY, LANES), F32),
            pltpu.VMEM((8, TILES // 2 * 8, LANES), F32),
        ],
        compiler_params=pltpu.CompilerParams(vmem_limit_bytes=VMEM_LIMIT),
        name="middle",
    )(norm, arrived, *grams, *table_in, *table_out)


def backward_y_kernel(in_ref, s_ref, maps_ref, gather_ref, high_ref, low_ref, kept_ref, sent_ref):
    core = lax.axis_index("core")
    block = BLOCK + 8
    curve = jnp.sum(in_ref[pl.ds(BLOCK, SLABS, stride=block), :], axis=0, keepdims=True)
    norm = jnp.sum(in_ref[pl.ds(BLOCK + 1, SLABS, stride=block), :], axis=0, keepdims=True)
    sums = jnp.where(lax.broadcasted_iota(jnp.int32, (8, LANES), 0) == 0, curve, norm)
    sums = jnp.concatenate([sums] + [jnp.zeros_like(sums)] * (N // LANES - 1), axis=1)
    kept_ref[HALF_ROWS:, :] = sums
    sent_ref[HALF_ROWS:, :] = sums
    for g in range(ROWS // 4):
        highs, lows = [], []
        for p in range(2):
            rows = [4 * g + 2 * p + i for i in range(2)]
            pieces = [arrived_rows(in_ref, r, block) for r in rows]
            done = transform(high_ref, low_ref, pieces, [times_i(x) for x in pieces])
            for i in range(2):
                back = done[:, LANES * i:LANES * (i + 1)]
                maps = dot(s_ref[rows[i]], maps_ref[...])
                high, low = split(maps[:, :LANES] * back - maps[:, LANES:] * times_i(back))
                highs.append(high)
                lows.append(low)
        total = dot(jnp.concatenate(highs + lows, axis=1), gather_ref[...]).T
        for r in range(4):
            a = 4 * g + r
            at = a % PAIRS * 2 * PLANES
            rows = total[2 * PLANES * r:2 * PLANES * (r + 1), :]

            @pl.when(core == a // PAIRS)
            def _():
                kept_ref[at:at + 2 * PLANES, :] = rows

            @pl.when(core != a // PAIRS)
            def _():
                sent_ref[at:at + 2 * PLANES, :] = rows


def backward_y(arrived, maps, sel_maps, sel_gather, table):
    vmem = pl.BlockSpec(memory_space=pltpu.VMEM)
    half = jax.ShapeDtypeStruct((HALF_ROWS + 8, N), F32)
    return pl.pallas_call(
        backward_y_kernel,
        in_specs=[vmem] * 6,
        out_specs=[vmem, vmem],
        out_shape=[half, half],
        compiler_params=pltpu.CompilerParams(vmem_limit_bytes=VMEM_LIMIT),
        name="backward_y",
    )(arrived, maps, sel_maps, sel_gather, *table)


def gram_kernel(counts_ref, w_ref, out_ref):
    step = pl.program_id(0)
    owners = w_ref.shape[0]
    at = pl.multiple_of((lax.axis_index("x") * 2 + lax.axis_index("core")) * 8, 8)
    lane = lax.broadcasted_iota(jnp.int32, (8, SB), 1)
    for o in range(owners):
        rows = []
        for j in range(CAP):
            live = counts_ref[j, step * owners + o]
            rows.append(jnp.where(lane < live, w_ref[o, j, pl.ds(at, 8), :], 0.0))
        l_high, l_low = split(jnp.concatenate(rows, axis=0))
        r_high, r_low = split(w_ref[o].reshape(CAP * CELLS, SB))
        gram = dot_nt(jnp.concatenate([l_high, l_low], axis=1), jnp.concatenate([r_high, r_high], axis=1))
        gram = gram + dot_nt(l_high, r_low)
        for m in range(CAP // 2):
            first = gram[16 * m:16 * m + 8, LANES * m:LANES * (m + 1)]
            second = gram[16 * m + 8:16 * m + 16, LANES * m:LANES * (m + 1)]
            out_ref[o, 8 * m:8 * m + 8, :] = jnp.where(lane < CELLS, first, second)


def gram_rows(interp, counts):
    owners = 8
    return pl.pallas_call(
        gram_kernel,
        grid=(SLABS // owners,),
        in_specs=[pl.BlockSpec(memory_space=pltpu.SMEM), pl.BlockSpec((owners, CAP, CELLS, SB), lambda i: (i, 0, 0, 0))],
        out_specs=pl.BlockSpec((owners, 16, LANES), lambda i: (i, 0, 0)),
        out_shape=jax.ShapeDtypeStruct((SLABS, 16, LANES), F32),
        compiler_params=pltpu.CompilerParams(vmem_limit_bytes=VMEM_LIMIT),
        name="gram_rows",
    )(counts, interp)


def share_kernel(own_ref, a_ref, b_ref, c_ref, residual_ref, out_ref, part_ref, sums_ref):
    total = (own_ref[...] + a_ref[...]) + (b_ref[...] + c_ref[...])
    curvature = jnp.sum(total[HALF_ROWS:HALF_ROWS + 1, :LANES], axis=1, keepdims=True)
    norm_now = jnp.sum(total[HALF_ROWS + 1:HALF_ROWS + 2, :LANES], axis=1, keepdims=True)
    step = norm_now / curvature
    half = residual_ref[lax.axis_index("core")] - step * total[:HALF_ROWS]
    out_ref[...] = half
    square = jnp.sum((half * half).reshape(HALF_ROWS // 8, 8, N), axis=0)
    part = jnp.sum(square[:, :LANES] + square[:, LANES:2 * LANES] + square[:, 2 * LANES:], axis=0, keepdims=True)
    part_ref[...] = jnp.broadcast_to(part[None], part_ref.shape)
    sums_ref[...] = jnp.where(lax.broadcasted_iota(jnp.int32, (8, LANES), 0) == 0, step, norm_now)


def residual_share(own, others, residual):
    vmem = pl.BlockSpec(memory_space=pltpu.VMEM)
    return pl.pallas_call(
        share_kernel,
        in_specs=[vmem] * 5,
        out_specs=[vmem] * 3,
        out_shape=[
            jax.ShapeDtypeStruct((HALF_ROWS, N), F32),
            jax.ShapeDtypeStruct((2 * SLABS, 1, LANES), F32),
            jax.ShapeDtypeStruct((8, LANES), F32),
        ],
        compiler_params=pltpu.CompilerParams(vmem_limit_bytes=VMEM_LIMIT),
        name="residual_share",
    )(own, *others, residual)


def image_kernel(sums_ref, image_ref, direction_ref, out_ref):
    out_ref[...] = image_ref[...] + sums_ref[0:1, 0:1] * direction_ref[...]


def image_update(sums, image, direction):
    vmem = pl.BlockSpec(memory_space=pltpu.VMEM)
    return pl.pallas_call(
        image_kernel,
        in_specs=[vmem] * 3,
        out_specs=vmem,
        out_shape=jax.ShapeDtypeStruct(image.shape, F32),
        name="image_update",
    )(sums, image, direction)


def finish_kernel(sums_ref, parts_ref, direction_ref, own_ref, other_ref, residual_ref, next_ref):
    ratio = jnp.sum(jnp.sum(parts_ref[...], axis=0), axis=1, keepdims=True) / sums_ref[1:2, 0:1]
    core = lax.axis_index("core")
    for half, ref in ((core, own_ref), (1 - core, other_ref)):
        residual_ref[half] = ref[...]
        next_ref[half] = ref[...] + ratio * direction_ref[half]


def finish(sums, parts, direction, own, other):
    vmem = pl.BlockSpec(memory_space=pltpu.VMEM)
    full = jax.ShapeDtypeStruct(direction.shape, F32)
    return pl.pallas_call(
        finish_kernel,
        in_specs=[vmem] * 5,
        out_specs=[vmem, vmem],
        out_shape=[full, full],
        compiler_params=pltpu.CompilerParams(vmem_limit_bytes=VMEM_LIMIT),
        name="finish",
    )(sums, parts, direction, own, other)


def swap_core(value):
    return lax.ppermute(value, "core", [(0, 1), (1, 0)])


def from_x(value):
    return [lax.ppermute(value, "x", [(i, (i + d) % 4) for i in range(4)]) for d in range(1, 4)]


def body(image_x, residual, direction, sensitivity, interp, slot_tile, counts):
    sending, arrival = ([tuple(jnp.asarray(t) for t in pair) for pair in pairs] for pairs in dft_tables())
    sel_maps, sel_spread, sel_gather = (jnp.asarray(t) for t in selections())
    image_t, residual_t, direction_t = (jnp.transpose(a, (0, 2, 1)) for a in (image_x, residual, direction))

    grams = gram_rows(interp[0], counts[0].T)
    grams = lax.all_to_all(grams, SLAB, split_axis=0, concat_axis=0, tiled=True)
    grams = gram_sum(grams, slot_tile[0].T)
    grams = [grams] + from_x(grams)
    grams = grams + [swap_core(g) for g in grams]

    outgoing = forward_y(direction_t, sensitivity, sel_maps, sel_spread, sending[0])
    pencils = lax.all_to_all(outgoing, SLAB, split_axis=0, concat_axis=0, tiled=True)
    norm = jnp.sum(residual_t * residual_t).reshape(1, 1)
    outgoing = middle(norm, pencils.reshape(-1, LANES), grams, arrival[0], sending[1])
    slab_rows = lax.all_to_all(outgoing, SLAB, split_axis=0, concat_axis=0, tiled=True)
    kept, sent = backward_y(slab_rows.reshape(-1, LANES), sensitivity, sel_maps, sel_gather, arrival[1])

    kept = kept + swap_core(sent)
    halves = (2, HALF_ROWS, N)
    half, parts, sums = residual_share(kept, from_x(kept), residual_t.reshape(halves))
    parts = lax.all_to_all(parts, SLAB + ("core",), split_axis=0, concat_axis=0, tiled=True)
    next_image = image_update(sums, image_t.reshape(halves), direction_t.reshape(halves))
    next_residual, next_direction = finish(sums, parts, direction_t.reshape(halves), half, swap_core(half))
    return tuple(
        jnp.transpose(a.reshape(direction_t.shape), (0, 2, 1)) for a in (next_image, next_residual, next_direction)
    )


def solution(mesh):
    fine = Mesh(mesh.devices.reshape(8, 4, 4, 2), ALL)
    rows = P(SLAB, None, None)
    return jax.shard_map(
        body,
        mesh=fine,
        in_specs=(
            rows,
            rows,
            rows,
            P(SLAB, None, COIL),
            P(SLAB, None, None, None, None),
            rows,
            rows,
        ),
        out_specs=(rows, rows, rows),
        check_vma=False,
    )
```

```python
import jax
import jax.numpy as jnp
import ml_dtypes
import numpy as np
from jax import lax
from jax.experimental import pallas as pl
from jax.experimental.pallas import tpu as pltpu
from jax.sharding import Mesh
from jax.sharding import PartitionSpec as P

N = 384
SLABS = 32
ROWS = 12
PAIRS = ROWS // 2
LANES = 128
PLANES = 16
TX = 16
TY = 4
CELLS = TX * TY
TILES = 72
CAP = 4
SB = 128
SLAB = ("z", "y")
COIL = ("x", "core")
ALL = ("z", "y", "x", "core")
HALF_ROWS = PAIRS * 2 * PLANES
QUARTER = HALF_ROWS // 2
BLOCK = 24 * PAIRS
HALF = LANES // 2
COILS = HALF // PLANES
VMEM_LIMIT = 56 * 1024 * 1024
F32 = jnp.float32
BF16 = jnp.bfloat16
NT = (((1,), (1,)), ((), ()))


def split_table(table):
    table = table.astype(np.float32)
    high = table.astype(ml_dtypes.bfloat16)
    low = (table - high.astype(np.float32)).astype(ml_dtypes.bfloat16)
    return high, low


def dft_tables():
    pos = np.arange(N)
    phase = (pos[:, None] * pos[None, :] % N) * (2.0 * np.pi / N)
    real = np.cos(phase) / np.sqrt(N)
    imag = -np.sin(phase) / np.sqrt(N)
    base = ROWS * np.arange(SLABS)[:, None]
    rows = np.concatenate([(base + np.arange(8)).reshape(-1), (base + np.arange(8, ROWS)).reshape(-1)])
    cols = np.concatenate([base.reshape(-1) + 2 * p + i for i in range(2) for p in range(PAIRS)])
    sending = [split_table(np.concatenate([real[rows], sign * imag[rows]], axis=1)) for sign in (1, -1)]
    arrival = [split_table(np.concatenate([real[:, cols], sign * imag[:, cols]], axis=1)) for sign in (1, -1)]
    return sending, arrival


def selections():
    place = np.arange(LANES)
    part, coil, plane = place // HALF, place // PLANES % COILS, place % PLANES
    group, src_part, src_plane = place // (2 * PLANES), place // PLANES % 2, place % PLANES
    same = (group[:, None] == coil) & (src_plane[:, None] == plane)
    maps = np.concatenate([same & (src_part[:, None] == 0), same & (src_part[:, None] == 1)], axis=1)
    spread, gather = [], []
    for r in range(4):
        hit = (group[:, None] == r) & (src_plane[:, None] == plane)
        from_real = hit & (src_part[:, None] == 0)
        from_imag = hit & (src_part[:, None] == 1)
        spread.append((from_real & (part == 0)) + (from_imag & (part == 1)) + 0.0)
        spread.append((from_real & (part == 1)) + 0.0 - (from_imag & (part == 0)))
        gather.append((group == r) & (src_plane == plane[:, None]) & (src_part == part[:, None]))
    spread = np.concatenate([np.concatenate(spread, axis=1)] * 2, axis=0)
    gather = np.concatenate(gather * 2, axis=0)
    return tuple(a.astype(ml_dtypes.bfloat16) for a in (maps, spread, gather))


def split(value):
    high = value.astype(BF16)
    return high, (value - high.astype(F32)).astype(BF16)


def dot(a, b):
    return jnp.dot(a, b, preferred_element_type=F32)


def dot_nt(a, b):
    return lax.dot_general(a, b, NT, preferred_element_type=F32)


def whole(array):
    return pl.BlockSpec(array.shape, lambda i: (0,) * array.ndim)


def times_i(value):
    rolled = pltpu.roll(value, HALF, 1)
    return jnp.where(lax.broadcasted_iota(jnp.int32, value.shape, 1) < HALF, -rolled, rolled)


def transform(high_ref, low_ref, pieces, turned):
    highs, lows = [], []
    for piece, turn in zip(pieces, turned):
        piece_high, piece_low = split(piece)
        turn_high, turn_low = split(turn)
        highs.append(jnp.concatenate([piece_high, turn_high], axis=0))
        lows.append(jnp.concatenate([piece_low, turn_low], axis=0))
    high = jnp.concatenate(highs, axis=1)
    low = jnp.concatenate(lows, axis=1)
    return dot(high_ref[...], high) + (dot(high_ref[...], low) + dot(low_ref[...], high))


def store_outgoing(out_ref, start, even, odd):
    out_ref[:, start:start + 8, :] = even[:256].reshape(SLABS, 8, LANES)
    out_ref[:, start + 8:start + 16, :] = odd[:256].reshape(SLABS, 8, LANES)
    lower = lax.broadcasted_iota(jnp.int32, (8, LANES), 0) < 4
    for m in range(SLABS // 2):
        first = even[256 + 8 * m:264 + 8 * m]
        second = odd[256 + 8 * m:264 + 8 * m]
        out_ref[2 * m, start + 16:start + 24, :] = jnp.where(lower, first, pltpu.roll(second, 4, 0))
        out_ref[2 * m + 1, start + 16:start + 24, :] = jnp.where(lower, pltpu.roll(first, 4, 0), second)


def gram_sum_kernel(tiles_ref, in_ref, out_ref, total):
    total[...] = jnp.zeros_like(total)
    lane = lax.broadcasted_iota(jnp.int32, (8, LANES), 1)

    def add(r, carry):
        for j in range(CAP):
            tile = tiles_ref[j, r]
            piece = in_ref[r, 8 * (j // 2):8 * (j // 2) + 8, :]
            keep = lane < CELLS if j % 2 == 0 else lane >= CELLS
            total[tile] = total[tile] + jnp.where(keep, piece, 0.0)
        return carry

    lax.fori_loop(0, SLABS, add, 0)
    groups = N // TX // 2
    for b in range(ROWS // TY):
        for m in range(groups):
            first = total[2 * m * 3 + b]
            second = total[(2 * m + 1) * 3 + b]
            first = first + pltpu.roll(first, CELLS, 1)
            second = second + pltpu.roll(second, CELLS, 1)
            at = (b * groups + m) * 8
            out_ref[at:at + 8, :] = jnp.where(lane < CELLS, first, second)


def gram_sum(arrived, tiles):
    return pl.pallas_call(
        gram_sum_kernel,
        in_specs=[pl.BlockSpec(memory_space=pltpu.SMEM), pl.BlockSpec(memory_space=pltpu.VMEM)],
        out_specs=pl.BlockSpec(memory_space=pltpu.VMEM),
        out_shape=jax.ShapeDtypeStruct((TILES // 2 * 8, LANES), F32),
        scratch_shapes=[pltpu.VMEM((TILES, 8, LANES), F32)],
        compiler_params=pltpu.CompilerParams(vmem_limit_bytes=VMEM_LIMIT),
        name="gram_sum",
    )(tiles, arrived)


def forward_y_kernel(d_ref, s_ref, maps_ref, spread_ref, high_ref, low_ref, out_ref):
    flipped = d_ref[...].reshape(LANES, N).T
    wide = dot(jnp.concatenate(split(flipped), axis=1), spread_ref[...])
    for p in range(2):
        images, turned = [], []
        for r in (2 * p, 2 * p + 1):
            maps = dot(s_ref[r], maps_ref[...])
            real_map, imag_map = maps[:, :LANES], maps[:, LANES:]
            d = wide[:, 2 * r * LANES:(2 * r + 1) * LANES]
            turned_d = wide[:, (2 * r + 1) * LANES:(2 * r + 2) * LANES]
            images.append(real_map * d + imag_map * turned_d)
            turned.append(real_map * turned_d - imag_map * d)
        done = transform(high_ref, low_ref, images, turned)
        store_outgoing(out_ref, 24 * p, done[:, :LANES], done[:, LANES:])


def forward_y(direction, maps, sel_maps, sel_spread, table):
    return pl.pallas_call(
        forward_y_kernel,
        grid=(ROWS // 4,),
        in_specs=[
            pl.BlockSpec((4, 2 * PLANES, N), lambda i: (i, 0, 0)),
            pl.BlockSpec((4, N, LANES), lambda i: (i, 0, 0)),
            whole(sel_maps),
            whole(sel_spread),
            whole(table[0]),
            whole(table[1]),
        ],
        out_specs=pl.BlockSpec((SLABS, 48, LANES), lambda i: (0, i, 0)),
        out_shape=jax.ShapeDtypeStruct((SLABS, 24 * PAIRS, LANES), F32),
        compiler_params=pltpu.CompilerParams(vmem_limit_bytes=VMEM_LIMIT),
        name="forward_y",
    )(direction, maps, sel_maps, sel_spread, *table)


def arrived_rows(ref, index, block):
    parts = []
    for i in range(2):
        start = i * 8 + index if index < 8 else 16 + 4 * i + index - 8
        parts += [ref[pl.ds(start + 24 * p, SLABS, stride=block), :] for p in range(PAIRS)]
    return jnp.concatenate(parts, axis=0)


def middle_kernel(norm_ref, in_hbm, *rest):
    g_hbm, tables_hbm = rest[:8], rest[8:12]
    out_hbm, in_ref, table_ref, g_ref, grid_ref, out_ref, in_sem, table_sem, g_sem, out_sem = rest[12:]
    fh_ref, fl_ref, bh_ref, bl_ref = (table_ref.at[i] for i in range(4))
    xpos, core = lax.axis_index("x"), lax.axis_index("core")
    load_in = pltpu.make_async_copy(in_hbm, in_ref, in_sem)
    load_tables = [pltpu.make_async_copy(tables_hbm[i], table_ref.at[i], table_sem.at[i]) for i in range(4)]
    load_g = []
    for d in range(4):
        for k in range(2):
            c = 2 * lax.rem(xpos + 4 - d, 4) + lax.rem(core + k, 2)
            load_g.append(pltpu.make_async_copy(g_hbm[4 * k + d], g_ref.at[c], g_sem.at[4 * k + d]))
    for copy in [load_in] + load_tables[:2] + load_g + load_tables[2:]:
        copy.start()
    for copy in [load_in] + load_tables[:2]:
        copy.wait()
    for p in range(PAIRS):
        pieces = [arrived_rows(in_ref, 2 * p + i, BLOCK) for i in range(2)]
        done = transform(fh_ref, fl_ref, pieces, [times_i(x) for x in pieces])
        for i in range(2):
            b = 2 * p + i
            grid_ref[b // TY, pl.ds(b % TY, N, stride=TY), :] = done[:, LANES * i:LANES * (i + 1)]
    for copy in load_g + load_tables[2:]:
        copy.wait()
    left = lax.broadcasted_iota(jnp.int32, (CELLS, LANES), 1) < CELLS
    curve = jnp.zeros((8, LANES), F32)
    groups = N // TX // 2
    for b in range(ROWS // TY):
        for m in range(groups):
            at = (b * groups + m) * 8
            packed = jnp.concatenate([g_ref[c, at:at + 8, :] for c in range(8)], axis=0)
            weights = jnp.concatenate([jnp.where(left, packed, 0.0), jnp.where(left, 0.0, packed)], axis=0)
            cells = slice(2 * m * CELLS, (2 * m + 2) * CELLS)
            tile = grid_ref[b, cells, :]
            w_high, w_low = split(weights)
            t_high, t_low = split(tile)
            applied = dot(jnp.concatenate([w_high, w_low], axis=1), jnp.concatenate([t_high, t_high], axis=0))
            applied = applied + dot(w_high, t_low)
            curve = curve + jnp.sum((tile * applied).reshape(2 * CELLS // 8, 8, LANES), axis=0)
            grid_ref[b, cells, :] = applied
    norm = jnp.broadcast_to(norm_ref[...], (8, LANES)) / (8 * LANES)
    sums = jnp.where(lax.broadcasted_iota(jnp.int32, (8, LANES), 0) == 0, jnp.sum(curve, axis=0, keepdims=True), norm)
    out_ref[:, BLOCK:, :] = jnp.broadcast_to(sums[None], (SLABS, 8, LANES))
    stores = [pltpu.make_async_copy(out_ref.at[:, BLOCK:, :], out_hbm.at[:, BLOCK:, :], out_sem.at[PAIRS])]
    stores[0].start()
    for p in range(PAIRS):
        pieces = [grid_ref[b // TY, pl.ds(b % TY, N, stride=TY), :] for b in (2 * p, 2 * p + 1)]
        done = transform(bh_ref, bl_ref, pieces, [times_i(x) for x in pieces])
        store_outgoing(out_ref, 24 * p, done[:, :LANES], done[:, LANES:])
        rows = pl.ds(24 * p, 24)
        stores.append(pltpu.make_async_copy(out_ref.at[:, rows, :], out_hbm.at[:, rows, :], out_sem.at[p]))
        stores[-1].start()
    for copy in stores:
        copy.wait()


def middle(norm, arrived, grams, table_in, table_out):
    hbm = pl.BlockSpec(memory_space=pltpu.HBM)
    return pl.pallas_call(
        middle_kernel,
        in_specs=[pl.BlockSpec(memory_space=pltpu.VMEM)] + [hbm] * 13,
        out_specs=hbm,
        out_shape=jax.ShapeDtypeStruct((SLABS, BLOCK + 8, LANES), F32),
        scratch_shapes=[
            pltpu.VMEM((SLABS * BLOCK, LANES), F32),
            pltpu.VMEM((4, N, 2 * N), BF16),
            pltpu.VMEM((8, TILES // 2 * 8, LANES), F32),
            pltpu.VMEM((ROWS // TY, N * TY, LANES), F32),
            pltpu.VMEM((SLABS, BLOCK + 8, LANES), F32),
            pltpu.SemaphoreType.DMA,
            pltpu.SemaphoreType.DMA((4,)),
            pltpu.SemaphoreType.DMA((8,)),
            pltpu.SemaphoreType.DMA((PAIRS + 1,)),
        ],
        compiler_params=pltpu.CompilerParams(vmem_limit_bytes=VMEM_LIMIT),
        name="middle",
    )(norm, arrived, *grams, *table_in, *table_out)


def backward_y_kernel(in_ref, s_ref, maps_ref, gather_ref, high_ref, low_ref, *rest):
    kept_refs, sent_refs = rest[:2], rest[2:]
    core = lax.axis_index("core")
    block = BLOCK + 8
    curve = jnp.sum(in_ref[pl.ds(BLOCK, SLABS, stride=block), :], axis=0, keepdims=True)
    norm = jnp.sum(in_ref[pl.ds(BLOCK + 1, SLABS, stride=block), :], axis=0, keepdims=True)
    sums = jnp.where(lax.broadcasted_iota(jnp.int32, (8, LANES), 0) == 0, curve, norm)
    sums = jnp.concatenate([sums] + [jnp.zeros_like(sums)] * (N // LANES - 1), axis=1)
    kept_refs[0][QUARTER:, :] = sums
    sent_refs[0][QUARTER:, :] = sums
    for g in range(ROWS // 4):
        highs, lows = [], []
        for p in range(2):
            rows = [4 * g + 2 * p + i for i in range(2)]
            pieces = [arrived_rows(in_ref, r, block) for r in rows]
            done = transform(high_ref, low_ref, pieces, [times_i(x) for x in pieces])
            for i in range(2):
                back = done[:, LANES * i:LANES * (i + 1)]
                maps = dot(s_ref[rows[i]], maps_ref[...])
                high, low = split(maps[:, :LANES] * back - maps[:, LANES:] * times_i(back))
                highs.append(high)
                lows.append(low)
        total = dot(jnp.concatenate(highs + lows, axis=1), gather_ref[...]).T
        for r in range(4):
            a = 4 * g + r
            at = a % (PAIRS // 2) * 2 * PLANES
            quarter = a // (PAIRS // 2) % 2
            rows = total[2 * PLANES * r:2 * PLANES * (r + 1), :]

            @pl.when(core == a // PAIRS)
            def _():
                kept_refs[quarter][at:at + 2 * PLANES, :] = rows

            @pl.when(core != a // PAIRS)
            def _():
                sent_refs[quarter][at:at + 2 * PLANES, :] = rows


def backward_y(arrived, maps, sel_maps, sel_gather, table):
    vmem = pl.BlockSpec(memory_space=pltpu.VMEM)
    quarters = [jax.ShapeDtypeStruct((QUARTER + 8, N), F32), jax.ShapeDtypeStruct((QUARTER, N), F32)]
    return pl.pallas_call(
        backward_y_kernel,
        in_specs=[vmem] * 6,
        out_specs=[vmem] * 4,
        out_shape=quarters * 2,
        compiler_params=pltpu.CompilerParams(vmem_limit_bytes=VMEM_LIMIT),
        name="backward_y",
    )(arrived, maps, sel_maps, sel_gather, *table)


def gram_kernel(counts_ref, w_ref, out_ref):
    step = pl.program_id(0)
    owners = w_ref.shape[0]
    at = pl.multiple_of((lax.axis_index("x") * 2 + lax.axis_index("core")) * 8, 8)
    lane = lax.broadcasted_iota(jnp.int32, (8, SB), 1)
    for o in range(owners):
        rows = []
        for j in range(CAP):
            live = counts_ref[j, step * owners + o]
            rows.append(jnp.where(lane < live, w_ref[o, j, pl.ds(at, 8), :], 0.0))
        l_high, l_low = split(jnp.concatenate(rows, axis=0))
        r_high, r_low = split(w_ref[o].reshape(CAP * CELLS, SB))
        gram = dot_nt(jnp.concatenate([l_high, l_low], axis=1), jnp.concatenate([r_high, r_high], axis=1))
        gram = gram + dot_nt(l_high, r_low)
        for m in range(CAP // 2):
            first = gram[16 * m:16 * m + 8, LANES * m:LANES * (m + 1)]
            second = gram[16 * m + 8:16 * m + 16, LANES * m:LANES * (m + 1)]
            out_ref[o, 8 * m:8 * m + 8, :] = jnp.where(lane < CELLS, first, second)


def gram_rows(interp, counts):
    owners = 16
    return pl.pallas_call(
        gram_kernel,
        grid=(SLABS // owners,),
        in_specs=[pl.BlockSpec(memory_space=pltpu.SMEM), pl.BlockSpec((owners, CAP, CELLS, SB), lambda i: (i, 0, 0, 0))],
        out_specs=pl.BlockSpec((owners, 16, LANES), lambda i: (i, 0, 0)),
        out_shape=jax.ShapeDtypeStruct((SLABS, 16, LANES), F32),
        compiler_params=pltpu.CompilerParams(vmem_limit_bytes=VMEM_LIMIT),
        name="gram_rows",
    )(counts, interp)


def share_kernel(a_ref, more_a_ref, b_ref, more_b_ref, residual_ref, out_ref, part_ref, sums_ref):
    first = a_ref[...] + more_a_ref[...]
    curvature = jnp.sum(first[QUARTER:QUARTER + 1, :LANES], axis=1, keepdims=True)
    norm_now = jnp.sum(first[QUARTER + 1:QUARTER + 2, :LANES], axis=1, keepdims=True)
    step = norm_now / curvature
    core = lax.axis_index("core")
    square = jnp.zeros((8, N), F32)
    for i, applied in enumerate((first[:QUARTER], b_ref[...] + more_b_ref[...])):
        rows = pl.ds(i * QUARTER, QUARTER)
        part = residual_ref[core, rows, :] - step * applied
        out_ref[rows, :] = part
        square = square + jnp.sum((part * part).reshape(QUARTER // 8, 8, N), axis=0)
    part = jnp.sum(square[:, :LANES] + square[:, LANES:2 * LANES] + square[:, 2 * LANES:], axis=0, keepdims=True)
    part_ref[...] = jnp.broadcast_to(part[None], part_ref.shape)
    sums_ref[...] = jnp.where(lax.broadcasted_iota(jnp.int32, (8, LANES), 0) == 0, step, norm_now)


def residual_share(first, second, residual):
    vmem = pl.BlockSpec(memory_space=pltpu.VMEM)
    return pl.pallas_call(
        share_kernel,
        in_specs=[vmem] * 5,
        out_specs=[vmem] * 3,
        out_shape=[
            jax.ShapeDtypeStruct((HALF_ROWS, N), F32),
            jax.ShapeDtypeStruct((2 * SLABS, 1, LANES), F32),
            jax.ShapeDtypeStruct((8, LANES), F32),
        ],
        compiler_params=pltpu.CompilerParams(vmem_limit_bytes=VMEM_LIMIT),
        name="residual_share",
    )(*first, *second, residual)


def image_kernel(sums_ref, image_ref, direction_ref, out_ref):
    out_ref[...] = image_ref[...] + sums_ref[0:1, 0:1] * direction_ref[...]


def image_update(sums, image, direction):
    vmem = pl.BlockSpec(memory_space=pltpu.VMEM)
    return pl.pallas_call(
        image_kernel,
        in_specs=[vmem] * 3,
        out_specs=vmem,
        out_shape=jax.ShapeDtypeStruct(image.shape, F32),
        name="image_update",
    )(sums, image, direction)


def finish_kernel(sums_ref, parts_ref, direction_ref, own_ref, other_ref, residual_ref, next_ref):
    ratio = jnp.sum(jnp.sum(parts_ref[...], axis=0), axis=1, keepdims=True) / sums_ref[1:2, 0:1]
    core = lax.axis_index("core")
    for half, ref in ((core, own_ref), (1 - core, other_ref)):
        residual_ref[half] = ref[...]
        next_ref[half] = ref[...] + ratio * direction_ref[half]


def finish(sums, parts, direction, own, other):
    vmem = pl.BlockSpec(memory_space=pltpu.VMEM)
    full = jax.ShapeDtypeStruct(direction.shape, F32)
    return pl.pallas_call(
        finish_kernel,
        in_specs=[vmem] * 5,
        out_specs=[vmem, vmem],
        out_shape=[full, full],
        compiler_params=pltpu.CompilerParams(vmem_limit_bytes=VMEM_LIMIT),
        name="finish",
    )(sums, parts, direction, own, other)


def swap_core(value):
    return lax.ppermute(value, "core", [(0, 1), (1, 0)])


def swap_x(value, mask):
    return lax.ppermute(value, "x", [(i, i ^ mask) for i in range(4)])


def from_x(value):
    return [lax.ppermute(value, "x", [(i, (i + d) % 4) for i in range(4)]) for d in range(1, 4)]


def body(image_x, residual, direction, sensitivity, interp, slot_tile, counts):
    sending, arrival = ([tuple(jnp.asarray(t) for t in pair) for pair in pairs] for pairs in dft_tables())
    sel_maps, sel_spread, sel_gather = (jnp.asarray(t) for t in selections())
    image_t, residual_t, direction_t = (jnp.transpose(a, (0, 2, 1)) for a in (image_x, residual, direction))

    grams = gram_rows(interp[0], counts[0].T)
    grams = lax.all_to_all(grams, SLAB, split_axis=0, concat_axis=0, tiled=True)
    grams = gram_sum(grams, slot_tile[0].T)
    grams = [grams] + from_x(grams)
    grams = grams + [swap_core(g) for g in grams]

    outgoing = forward_y(direction_t, sensitivity, sel_maps, sel_spread, sending[0])
    pencils = lax.all_to_all(outgoing, SLAB, split_axis=0, concat_axis=0, tiled=True)
    norm = jnp.sum(residual_t * residual_t).reshape(1, 1)
    outgoing = middle(norm, pencils.reshape(-1, LANES), grams, arrival[0], sending[1])
    slab_rows = lax.all_to_all(outgoing, SLAB, split_axis=0, concat_axis=0, tiled=True)
    kept_a, kept_b, sent_a, sent_b = backward_y(
        slab_rows.reshape(-1, LANES), sensitivity, sel_maps, sel_gather, arrival[1]
    )

    kept_a = kept_a + swap_core(sent_a)
    kept_b = kept_b + swap_core(sent_b)
    kept_a = kept_a + swap_x(kept_a, 1)
    kept_b = kept_b + swap_x(kept_b, 3)
    halves = (2, HALF_ROWS, N)
    half, parts, sums = residual_share(
        (kept_a, swap_x(kept_a, 3)), (kept_b, swap_x(kept_b, 1)), residual_t.reshape(halves)
    )
    parts = lax.all_to_all(parts, SLAB + ("core",), split_axis=0, concat_axis=0, tiled=True)
    next_image = image_update(sums, image_t.reshape(halves), direction_t.reshape(halves))
    next_residual, next_direction = finish(sums, parts, direction_t.reshape(halves), half, swap_core(half))
    return tuple(
        jnp.transpose(a.reshape(direction_t.shape), (0, 2, 1)) for a in (next_image, next_residual, next_direction)
    )


def solution(mesh):
    fine = Mesh(mesh.devices.reshape(8, 4, 4, 2), ALL)
    rows = P(SLAB, None, None)
    return jax.shard_map(
        body,
        mesh=fine,
        in_specs=(
            rows,
            rows,
            rows,
            P(SLAB, None, COIL),
            P(SLAB, None, None, None, None),
            rows,
            rows,
        ),
        out_specs=(rows, rows, rows),
        check_vma=False,
    )
```

```python
import jax
import jax.numpy as jnp
import ml_dtypes
import numpy as np
from jax import lax
from jax.experimental import pallas as pl
from jax.experimental.pallas import tpu as pltpu
from jax.sharding import Mesh
from jax.sharding import PartitionSpec as P

N = 384
SLABS = 32
ROWS = 12
PAIRS = ROWS // 2
LANES = 128
PLANES = 16
TX = 16
TY = 4
CELLS = TX * TY
TILES = 72
CAP = 4
SB = 128
SLAB = ("z", "y")
COIL = ("x", "core")
ALL = ("z", "y", "x", "core")
HALF_ROWS = PAIRS * 2 * PLANES
QUARTER = HALF_ROWS // 2
BLOCK = 24 * PAIRS
HALF = LANES // 2
COILS = HALF // PLANES
VMEM_LIMIT = 32 * 1024 * 1024
VMEM_ALL = 56 * 1024 * 1024
F32 = jnp.float32
BF16 = jnp.bfloat16
NT = (((1,), (1,)), ((), ()))


def split_table(table):
    table = table.astype(np.float32)
    high = table.astype(ml_dtypes.bfloat16)
    low = (table - high.astype(np.float32)).astype(ml_dtypes.bfloat16)
    return high, low


def dft_tables():
    pos = np.arange(N)
    phase = (pos[:, None] * pos[None, :] % N) * (2.0 * np.pi / N)
    real = np.cos(phase) / np.sqrt(N)
    imag = -np.sin(phase) / np.sqrt(N)
    base = ROWS * np.arange(SLABS)[:, None]
    rows = np.concatenate([(base + np.arange(8)).reshape(-1), (base + np.arange(8, ROWS)).reshape(-1)])
    cols = np.concatenate([base.reshape(-1) + 2 * p + i for i in range(2) for p in range(PAIRS)])
    sending = [split_table(np.concatenate([real[rows], sign * imag[rows]], axis=1)) for sign in (1, -1)]
    arrival = [split_table(np.concatenate([real[:, cols], sign * imag[:, cols]], axis=1)) for sign in (1, -1)]
    return sending, arrival


def selections():
    place = np.arange(LANES)
    part, coil, plane = place // HALF, place // PLANES % COILS, place % PLANES
    group, src_part, src_plane = place // (2 * PLANES), place // PLANES % 2, place % PLANES
    same = (group[:, None] == coil) & (src_plane[:, None] == plane)
    maps = np.concatenate([same & (src_part[:, None] == 0), same & (src_part[:, None] == 1)], axis=1)
    spread, gather = [], []
    for r in range(4):
        hit = (group[:, None] == r) & (src_plane[:, None] == plane)
        from_real = hit & (src_part[:, None] == 0)
        from_imag = hit & (src_part[:, None] == 1)
        spread.append((from_real & (part == 0)) + (from_imag & (part == 1)) + 0.0)
        spread.append((from_real & (part == 1)) + 0.0 - (from_imag & (part == 0)))
        gather.append((group == r) & (src_plane == plane[:, None]) & (src_part == part[:, None]))
    spread = np.concatenate([np.concatenate(spread, axis=1)] * 2, axis=0)
    gather = np.concatenate(gather * 2, axis=0)
    return tuple(a.astype(ml_dtypes.bfloat16) for a in (maps, spread, gather))


def split(value):
    high = value.astype(BF16)
    return high, (value - high.astype(F32)).astype(BF16)


def dot(a, b):
    return jnp.dot(a, b, preferred_element_type=F32)


def dot_nt(a, b):
    return lax.dot_general(a, b, NT, preferred_element_type=F32)


def near(*arrays):
    return [pltpu.with_memory_space_constraint(a, pltpu.VMEM) for a in arrays]


def far(*arrays):
    return [pltpu.with_memory_space_constraint(a, pltpu.HBM) for a in arrays]


def near_out(*shape):
    return pltpu.VMEM(shape, F32)


def whole(array):
    return pl.BlockSpec(array.shape, lambda i: (0,) * array.ndim)


def times_i(value):
    rolled = pltpu.roll(value, HALF, 1)
    return jnp.where(lax.broadcasted_iota(jnp.int32, value.shape, 1) < HALF, -rolled, rolled)


def transform(high_ref, low_ref, pieces, turned):
    highs, lows = [], []
    for piece, turn in zip(pieces, turned):
        piece_high, piece_low = split(piece)
        turn_high, turn_low = split(turn)
        highs.append(jnp.concatenate([piece_high, turn_high], axis=0))
        lows.append(jnp.concatenate([piece_low, turn_low], axis=0))
    high = jnp.concatenate(highs, axis=1)
    low = jnp.concatenate(lows, axis=1)
    return dot(high_ref[...], high) + (dot(high_ref[...], low) + dot(low_ref[...], high))


def store_outgoing(out_ref, start, even, odd):
    out_ref[:, start:start + 8, :] = even[:256].reshape(SLABS, 8, LANES)
    out_ref[:, start + 8:start + 16, :] = odd[:256].reshape(SLABS, 8, LANES)
    lower = lax.broadcasted_iota(jnp.int32, (8, LANES), 0) < 4
    for m in range(SLABS // 2):
        first = even[256 + 8 * m:264 + 8 * m]
        second = odd[256 + 8 * m:264 + 8 * m]
        out_ref[2 * m, start + 16:start + 24, :] = jnp.where(lower, first, pltpu.roll(second, 4, 0))
        out_ref[2 * m + 1, start + 16:start + 24, :] = jnp.where(lower, pltpu.roll(first, 4, 0), second)


def gram_sum_kernel(tiles_ref, in_ref, out_ref, total):
    total[...] = jnp.zeros_like(total)
    lane = lax.broadcasted_iota(jnp.int32, (8, LANES), 1)

    def add(r, carry):
        for j in range(CAP):
            tile = tiles_ref[j, r]
            piece = in_ref[r, 8 * (j // 2):8 * (j // 2) + 8, :]
            keep = lane < CELLS if j % 2 == 0 else lane >= CELLS
            total[tile] = total[tile] + jnp.where(keep, piece, 0.0)
        return carry

    lax.fori_loop(0, SLABS, add, 0)
    groups = N // TX // 2
    for b in range(ROWS // TY):
        for m in range(groups):
            first = total[2 * m * 3 + b]
            second = total[(2 * m + 1) * 3 + b]
            first = first + pltpu.roll(first, CELLS, 1)
            second = second + pltpu.roll(second, CELLS, 1)
            at = (b * groups + m) * 8
            out_ref[at:at + 8, :] = jnp.where(lane < CELLS, first, second)


def gram_sum(arrived, tiles):
    return pl.pallas_call(
        gram_sum_kernel,
        in_specs=[pl.BlockSpec(memory_space=pltpu.SMEM), pl.BlockSpec(memory_space=pltpu.VMEM)],
        out_specs=pl.BlockSpec(memory_space=pltpu.VMEM),
        out_shape=jax.ShapeDtypeStruct((TILES // 2 * 8, LANES), F32),
        scratch_shapes=[pltpu.VMEM((TILES, 8, LANES), F32)],
        compiler_params=pltpu.CompilerParams(vmem_limit_bytes=VMEM_LIMIT),
        name="gram_sum",
    )(tiles, arrived)


def forward_y_kernel(d_ref, s_ref, maps_ref, spread_ref, high_ref, low_ref, out_ref):
    flipped = d_ref[...].reshape(LANES, N).T
    wide = dot(jnp.concatenate(split(flipped), axis=1), spread_ref[...])
    for p in range(2):
        images, turned = [], []
        for r in (2 * p, 2 * p + 1):
            maps = dot(s_ref[r], maps_ref[...])
            real_map, imag_map = maps[:, :LANES], maps[:, LANES:]
            d = wide[:, 2 * r * LANES:(2 * r + 1) * LANES]
            turned_d = wide[:, (2 * r + 1) * LANES:(2 * r + 2) * LANES]
            images.append(real_map * d + imag_map * turned_d)
            turned.append(real_map * turned_d - imag_map * d)
        done = transform(high_ref, low_ref, images, turned)
        store_outgoing(out_ref, 24 * p, done[:, :LANES], done[:, LANES:])


def forward_y(direction, maps, sel_maps, sel_spread, table):
    return pl.pallas_call(
        forward_y_kernel,
        grid=(ROWS // 4,),
        in_specs=[
            pl.BlockSpec((4, 2 * PLANES, N), lambda i: (i, 0, 0)),
            pl.BlockSpec((4, N, LANES), lambda i: (i, 0, 0)),
            whole(sel_maps),
            whole(sel_spread),
            whole(table[0]),
            whole(table[1]),
        ],
        out_specs=pl.BlockSpec((SLABS, 48, LANES), lambda i: (0, i, 0)),
        out_shape=jax.ShapeDtypeStruct((SLABS, 24 * PAIRS, LANES), F32),
        compiler_params=pltpu.CompilerParams(vmem_limit_bytes=VMEM_LIMIT),
        name="forward_y",
    )(direction, maps, sel_maps, sel_spread, *table)


def arrived_rows(ref, index, block):
    parts = []
    for i in range(2):
        start = i * 8 + index if index < 8 else 16 + 4 * i + index - 8
        parts += [ref[pl.ds(start + 24 * p, SLABS, stride=block), :] for p in range(PAIRS)]
    return jnp.concatenate(parts, axis=0)


def middle_kernel(norm_ref, in_ref, *rest):
    g_hbm, tables_hbm = rest[:8], rest[8:12]
    out_ref, table_ref, g_ref, grid_ref, table_sem, g_sem = rest[12:]
    fh_ref, fl_ref, bh_ref, bl_ref = (table_ref.at[i] for i in range(4))
    xpos, core = lax.axis_index("x"), lax.axis_index("core")
    load_tables = [pltpu.make_async_copy(tables_hbm[i], table_ref.at[i], table_sem.at[i]) for i in range(4)]
    load_g = []
    for d in range(4):
        for k in range(2):
            c = 2 * lax.rem(xpos + 4 - d, 4) + lax.rem(core + k, 2)
            load_g.append(pltpu.make_async_copy(g_hbm[4 * k + d], g_ref.at[c], g_sem.at[4 * k + d]))
    for copy in load_tables[:2] + load_g + load_tables[2:]:
        copy.start()
    for copy in load_tables[:2]:
        copy.wait()
    for p in range(PAIRS):
        pieces = [arrived_rows(in_ref, 2 * p + i, BLOCK) for i in range(2)]
        done = transform(fh_ref, fl_ref, pieces, [times_i(x) for x in pieces])
        for i in range(2):
            b = 2 * p + i
            grid_ref[b // TY, pl.ds(b % TY, N, stride=TY), :] = done[:, LANES * i:LANES * (i + 1)]
    for copy in load_g + load_tables[2:]:
        copy.wait()
    left = lax.broadcasted_iota(jnp.int32, (CELLS, LANES), 1) < CELLS
    curve = jnp.zeros((8, LANES), F32)
    groups = N // TX // 2
    for b in range(ROWS // TY):
        for m in range(groups):
            at = (b * groups + m) * 8
            packed = jnp.concatenate([g_ref[c, at:at + 8, :] for c in range(8)], axis=0)
            weights = jnp.concatenate([jnp.where(left, packed, 0.0), jnp.where(left, 0.0, packed)], axis=0)
            cells = slice(2 * m * CELLS, (2 * m + 2) * CELLS)
            tile = grid_ref[b, cells, :]
            w_high, w_low = split(weights)
            t_high, t_low = split(tile)
            applied = dot(jnp.concatenate([w_high, w_low], axis=1), jnp.concatenate([t_high, t_high], axis=0))
            applied = applied + dot(w_high, t_low)
            curve = curve + jnp.sum((tile * applied).reshape(2 * CELLS // 8, 8, LANES), axis=0)
            grid_ref[b, cells, :] = applied
    norm = jnp.broadcast_to(norm_ref[...], (8, LANES)) / (8 * LANES)
    sums = jnp.where(lax.broadcasted_iota(jnp.int32, (8, LANES), 0) == 0, jnp.sum(curve, axis=0, keepdims=True), norm)
    out_ref[:, BLOCK:, :] = jnp.broadcast_to(sums[None], (SLABS, 8, LANES))
    for p in range(PAIRS):
        pieces = [grid_ref[b // TY, pl.ds(b % TY, N, stride=TY), :] for b in (2 * p, 2 * p + 1)]
        done = transform(bh_ref, bl_ref, pieces, [times_i(x) for x in pieces])
        store_outgoing(out_ref, 24 * p, done[:, :LANES], done[:, LANES:])


def middle(norm, arrived, grams, table_in, table_out):
    vmem = pl.BlockSpec(memory_space=pltpu.VMEM)
    hbm = pl.BlockSpec(memory_space=pltpu.HBM)
    return pl.pallas_call(
        middle_kernel,
        in_specs=[vmem] * 2 + [hbm] * 12,
        out_specs=vmem,
        out_shape=near_out(SLABS, BLOCK + 8, LANES),
        scratch_shapes=[
            pltpu.VMEM((4, N, 2 * N), BF16),
            pltpu.VMEM((8, TILES // 2 * 8, LANES), F32),
            pltpu.VMEM((ROWS // TY, N * TY, LANES), F32),
            pltpu.SemaphoreType.DMA((4,)),
            pltpu.SemaphoreType.DMA((8,)),
        ],
        compiler_params=pltpu.CompilerParams(vmem_limit_bytes=VMEM_LIMIT),
        name="middle",
    )(norm, *near(arrived), *far(*grams, *table_in, *table_out))


def backward_y_kernel(in_ref, s_ref, maps_ref, gather_ref, high_ref, low_ref, *rest):
    kept_refs, sent_refs = rest[:2], rest[2:]
    core = lax.axis_index("core")
    block = BLOCK + 8
    curve = jnp.sum(in_ref[pl.ds(BLOCK, SLABS, stride=block), :], axis=0, keepdims=True)
    norm = jnp.sum(in_ref[pl.ds(BLOCK + 1, SLABS, stride=block), :], axis=0, keepdims=True)
    sums = jnp.where(lax.broadcasted_iota(jnp.int32, (8, LANES), 0) == 0, curve, norm)
    sums = jnp.concatenate([sums] + [jnp.zeros_like(sums)] * (N // LANES - 1), axis=1)
    kept_refs[0][QUARTER:, :] = sums
    sent_refs[0][QUARTER:, :] = sums
    for g in range(ROWS // 4):
        highs, lows = [], []
        for p in range(2):
            rows = [4 * g + 2 * p + i for i in range(2)]
            pieces = [arrived_rows(in_ref, r, block) for r in rows]
            done = transform(high_ref, low_ref, pieces, [times_i(x) for x in pieces])
            for i in range(2):
                back = done[:, LANES * i:LANES * (i + 1)]
                maps = dot(s_ref[rows[i]], maps_ref[...])
                high, low = split(maps[:, :LANES] * back - maps[:, LANES:] * times_i(back))
                highs.append(high)
                lows.append(low)
        total = dot(jnp.concatenate(highs + lows, axis=1), gather_ref[...]).T
        for r in range(4):
            a = 4 * g + r
            at = a % (PAIRS // 2) * 2 * PLANES
            quarter = a // (PAIRS // 2) % 2
            rows = total[2 * PLANES * r:2 * PLANES * (r + 1), :]

            @pl.when(core == a // PAIRS)
            def _():
                kept_refs[quarter][at:at + 2 * PLANES, :] = rows

            @pl.when(core != a // PAIRS)
            def _():
                sent_refs[quarter][at:at + 2 * PLANES, :] = rows


def backward_y(arrived, maps, sel_maps, sel_gather, table):
    vmem = pl.BlockSpec(memory_space=pltpu.VMEM)
    quarters = [near_out(QUARTER + 8, N), near_out(QUARTER, N)]
    return pl.pallas_call(
        backward_y_kernel,
        in_specs=[vmem] * 6,
        out_specs=[vmem] * 4,
        out_shape=quarters * 2,
        compiler_params=pltpu.CompilerParams(vmem_limit_bytes=VMEM_LIMIT),
        name="backward_y",
    )(*near(arrived, maps, sel_maps, sel_gather, *table))


def gram_kernel(counts_ref, w_ref, out_ref):
    step = pl.program_id(0)
    owners = w_ref.shape[0]
    at = pl.multiple_of((lax.axis_index("x") * 2 + lax.axis_index("core")) * 8, 8)
    lane = lax.broadcasted_iota(jnp.int32, (8, SB), 1)
    for o in range(owners):
        rows = []
        for j in range(CAP):
            live = counts_ref[j, step * owners + o]
            rows.append(jnp.where(lane < live, w_ref[o, j, pl.ds(at, 8), :], 0.0))
        l_high, l_low = split(jnp.concatenate(rows, axis=0))
        r_high, r_low = split(w_ref[o].reshape(CAP * CELLS, SB))
        gram = dot_nt(jnp.concatenate([l_high, l_low], axis=1), jnp.concatenate([r_high, r_high], axis=1))
        gram = gram + dot_nt(l_high, r_low)
        for m in range(CAP // 2):
            first = gram[16 * m:16 * m + 8, LANES * m:LANES * (m + 1)]
            second = gram[16 * m + 8:16 * m + 16, LANES * m:LANES * (m + 1)]
            out_ref[o, 8 * m:8 * m + 8, :] = jnp.where(lane < CELLS, first, second)


def gram_rows(interp, counts):
    owners = 16
    return pl.pallas_call(
        gram_kernel,
        grid=(SLABS // owners,),
        in_specs=[pl.BlockSpec(memory_space=pltpu.SMEM), pl.BlockSpec((owners, CAP, CELLS, SB), lambda i: (i, 0, 0, 0))],
        out_specs=pl.BlockSpec((owners, 16, LANES), lambda i: (i, 0, 0)),
        out_shape=jax.ShapeDtypeStruct((SLABS, 16, LANES), F32),
        compiler_params=pltpu.CompilerParams(vmem_limit_bytes=VMEM_ALL),
        name="gram_rows",
    )(counts, *far(interp))


def share_kernel(a_ref, more_a_ref, b_ref, more_b_ref, residual_ref, out_ref, part_ref, sums_ref):
    first = a_ref[...] + more_a_ref[...]
    curvature = jnp.sum(first[QUARTER:QUARTER + 1, :LANES], axis=1, keepdims=True)
    norm_now = jnp.sum(first[QUARTER + 1:QUARTER + 2, :LANES], axis=1, keepdims=True)
    step = norm_now / curvature
    core = lax.axis_index("core")
    square = jnp.zeros((8, N), F32)
    for i, applied in enumerate((first[:QUARTER], b_ref[...] + more_b_ref[...])):
        rows = pl.ds(i * QUARTER, QUARTER)
        part = residual_ref[core, rows, :] - step * applied
        out_ref[rows, :] = part
        square = square + jnp.sum((part * part).reshape(QUARTER // 8, 8, N), axis=0)
    part = jnp.sum(square[:, :LANES] + square[:, LANES:2 * LANES] + square[:, 2 * LANES:], axis=0, keepdims=True)
    part_ref[...] = jnp.broadcast_to(part[None], part_ref.shape)
    sums_ref[...] = jnp.where(lax.broadcasted_iota(jnp.int32, (8, LANES), 0) == 0, step, norm_now)


def residual_share(first, second, residual):
    vmem = pl.BlockSpec(memory_space=pltpu.VMEM)
    return pl.pallas_call(
        share_kernel,
        in_specs=[vmem] * 5,
        out_specs=[vmem] * 3,
        out_shape=[
            near_out(HALF_ROWS, N),
            near_out(2 * SLABS, 1, LANES),
            near_out(8, LANES),
        ],
        compiler_params=pltpu.CompilerParams(vmem_limit_bytes=VMEM_LIMIT),
        name="residual_share",
    )(*near(*first, *second, residual))


def image_kernel(sums_ref, image_ref, direction_ref, out_ref):
    out_ref[...] = image_ref[...] + sums_ref[0:1, 0:1] * direction_ref[...]


def image_update(sums, image, direction):
    vmem = pl.BlockSpec(memory_space=pltpu.VMEM)
    return pl.pallas_call(
        image_kernel,
        in_specs=[vmem] * 3,
        out_specs=vmem,
        out_shape=jax.ShapeDtypeStruct(image.shape, F32),
        name="image_update",
    )(*near(sums, image, direction))


def finish_kernel(sums_ref, parts_ref, direction_ref, own_ref, other_ref, residual_ref, next_ref):
    ratio = jnp.sum(jnp.sum(parts_ref[...], axis=0), axis=1, keepdims=True) / sums_ref[1:2, 0:1]
    core = lax.axis_index("core")
    for half, ref in ((core, own_ref), (1 - core, other_ref)):
        residual_ref[half] = ref[...]
        next_ref[half] = ref[...] + ratio * direction_ref[half]


def finish(sums, parts, direction, own, other):
    vmem = pl.BlockSpec(memory_space=pltpu.VMEM)
    full = jax.ShapeDtypeStruct(direction.shape, F32)
    return pl.pallas_call(
        finish_kernel,
        in_specs=[vmem] * 5,
        out_specs=[vmem, vmem],
        out_shape=[full, full],
        compiler_params=pltpu.CompilerParams(vmem_limit_bytes=VMEM_LIMIT),
        name="finish",
    )(*near(sums, parts, direction, own, other))


def swap_core(value):
    return lax.ppermute(value, "core", [(0, 1), (1, 0)])


def swap_x(value, mask):
    return lax.ppermute(value, "x", [(i, i ^ mask) for i in range(4)])


def from_x(value):
    return [lax.ppermute(value, "x", [(i, (i + d) % 4) for i in range(4)]) for d in range(1, 4)]


def body(image_x, residual, direction, sensitivity, interp, slot_tile, counts):
    sending, arrival = ([tuple(jnp.asarray(t) for t in pair) for pair in pairs] for pairs in dft_tables())
    sel_maps, sel_spread, sel_gather = (jnp.asarray(t) for t in selections())
    image_t, residual_t, direction_t = (jnp.transpose(a, (0, 2, 1)) for a in (image_x, residual, direction))

    grams = gram_rows(interp[0], counts[0].T)
    grams = lax.all_to_all(grams, SLAB, split_axis=0, concat_axis=0, tiled=True)
    grams = gram_sum(grams, slot_tile[0].T)
    grams = [grams] + from_x(grams)
    grams = grams + [swap_core(g) for g in grams]

    outgoing = forward_y(direction_t, sensitivity, sel_maps, sel_spread, sending[0])
    pencils = lax.all_to_all(outgoing, SLAB, split_axis=0, concat_axis=0, tiled=True)
    norm = jnp.sum(residual_t * residual_t).reshape(1, 1)
    outgoing = middle(norm, pencils.reshape(-1, LANES), grams, arrival[0], sending[1])
    slab_rows = lax.all_to_all(outgoing, SLAB, split_axis=0, concat_axis=0, tiled=True)
    kept_a, kept_b, sent_a, sent_b = backward_y(
        slab_rows.reshape(-1, LANES), sensitivity, sel_maps, sel_gather, arrival[1]
    )

    kept_a = kept_a + swap_core(sent_a)
    kept_b = kept_b + swap_core(sent_b)
    kept_a = kept_a + swap_x(kept_a, 1)
    kept_b = kept_b + swap_x(kept_b, 3)
    halves = (2, HALF_ROWS, N)
    half, parts, sums = residual_share(
        (kept_a, swap_x(kept_a, 3)), (kept_b, swap_x(kept_b, 1)), residual_t.reshape(halves)
    )
    parts = lax.all_to_all(parts, SLAB + ("core",), split_axis=0, concat_axis=0, tiled=True)
    next_image = image_update(sums, image_t.reshape(halves), direction_t.reshape(halves))
    next_residual, next_direction = finish(sums, parts, direction_t.reshape(halves), half, swap_core(half))
    return tuple(
        jnp.transpose(a.reshape(direction_t.shape), (0, 2, 1)) for a in (next_image, next_residual, next_direction)
    )


def solution(mesh):
    fine = Mesh(mesh.devices.reshape(8, 4, 4, 2), ALL)
    rows = P(SLAB, None, None)
    return jax.shard_map(
        body,
        mesh=fine,
        in_specs=(
            rows,
            rows,
            rows,
            P(SLAB, None, COIL),
            P(SLAB, None, None, None, None),
            rows,
            rows,
        ),
        out_specs=(rows, rows, rows),
        check_vma=False,
    )
```

```python
import jax
import jax.numpy as jnp
import ml_dtypes
import numpy as np
from jax import lax
from jax.experimental import pallas as pl
from jax.experimental.pallas import tpu as pltpu
from jax.sharding import Mesh
from jax.sharding import PartitionSpec as P

N = 384
SLABS = 32
ROWS = 12
PAIRS = ROWS // 2
LANES = 128
PLANES = 16
TX = 16
TY = 4
CELLS = TX * TY
TILES = 72
CAP = 4
SB = 128
SLAB = ("z", "y")
COIL = ("x", "core")
ALL = ("z", "y", "x", "core")
HALF_ROWS = PAIRS * 2 * PLANES
ZS = 8
YS = 4
QUARTER = HALF_ROWS // 2
BLOCK = 24 * PAIRS
HALF = LANES // 2
COILS = HALF // PLANES
VMEM_LIMIT = 32 * 1024 * 1024
VMEM_ALL = 56 * 1024 * 1024
F32 = jnp.float32
BF16 = jnp.bfloat16
NT = (((1,), (1,)), ((), ()))


def split_table(table):
    table = table.astype(np.float32)
    high = table.astype(ml_dtypes.bfloat16)
    low = (table - high.astype(np.float32)).astype(ml_dtypes.bfloat16)
    return high, low


def dft_tables():
    pos = np.arange(N)
    phase = (pos[:, None] * pos[None, :] % N) * (2.0 * np.pi / N)
    real = np.cos(phase) / np.sqrt(N)
    imag = -np.sin(phase) / np.sqrt(N)
    base = ROWS * np.arange(SLABS)[:, None]
    rows = np.concatenate([(base + np.arange(8)).reshape(-1), (base + np.arange(8, ROWS)).reshape(-1)])
    cols = np.concatenate([base.reshape(-1) + 2 * p + i for i in range(2) for p in range(PAIRS)])
    sending = [split_table(np.concatenate([real[rows], sign * imag[rows]], axis=1)) for sign in (1, -1)]
    arrival = [split_table(np.concatenate([real[:, cols], sign * imag[:, cols]], axis=1)) for sign in (1, -1)]
    return sending, arrival


def selections():
    place = np.arange(LANES)
    part, coil, plane = place // HALF, place // PLANES % COILS, place % PLANES
    group, src_part, src_plane = place // (2 * PLANES), place // PLANES % 2, place % PLANES
    same = (group[:, None] == coil) & (src_plane[:, None] == plane)
    maps = np.concatenate([same & (src_part[:, None] == 0), same & (src_part[:, None] == 1)], axis=1)
    spread, gather = [], []
    for r in range(4):
        hit = (group[:, None] == r) & (src_plane[:, None] == plane)
        from_real = hit & (src_part[:, None] == 0)
        from_imag = hit & (src_part[:, None] == 1)
        spread.append((from_real & (part == 0)) + (from_imag & (part == 1)) + 0.0)
        spread.append((from_real & (part == 1)) + 0.0 - (from_imag & (part == 0)))
        gather.append((group == r) & (src_plane == plane[:, None]) & (src_part == part[:, None]))
    spread = np.concatenate([np.concatenate(spread, axis=1)] * 2, axis=0)
    gather = np.concatenate(gather * 2, axis=0)
    return tuple(a.astype(ml_dtypes.bfloat16) for a in (maps, spread, gather))


def split(value):
    high = value.astype(BF16)
    return high, (value - high.astype(F32)).astype(BF16)


def dot(a, b):
    return jnp.dot(a, b, preferred_element_type=F32)


def dot_nt(a, b):
    return lax.dot_general(a, b, NT, preferred_element_type=F32)


def near(*arrays):
    return [pltpu.with_memory_space_constraint(a, pltpu.VMEM) for a in arrays]


def far(*arrays):
    return [pltpu.with_memory_space_constraint(a, pltpu.HBM) for a in arrays]


def near_out(*shape):
    return pltpu.VMEM(shape, F32)


def whole(array):
    return pl.BlockSpec(array.shape, lambda i: (0,) * array.ndim)


def times_i(value):
    rolled = pltpu.roll(value, HALF, 1)
    return jnp.where(lax.broadcasted_iota(jnp.int32, value.shape, 1) < HALF, -rolled, rolled)


def transform(high_ref, low_ref, pieces, turned):
    highs, lows = [], []
    for piece, turn in zip(pieces, turned):
        piece_high, piece_low = split(piece)
        turn_high, turn_low = split(turn)
        highs.append(jnp.concatenate([piece_high, turn_high], axis=0))
        lows.append(jnp.concatenate([piece_low, turn_low], axis=0))
    high = jnp.concatenate(highs, axis=1)
    low = jnp.concatenate(lows, axis=1)
    return dot(high_ref[...], high) + (dot(high_ref[...], low) + dot(low_ref[...], high))


def store_outgoing(out_ref, start, even, odd):
    out_ref[:, start:start + 8, :] = even[:256].reshape(SLABS, 8, LANES)
    out_ref[:, start + 8:start + 16, :] = odd[:256].reshape(SLABS, 8, LANES)
    lower = lax.broadcasted_iota(jnp.int32, (8, LANES), 0) < 4
    for m in range(SLABS // 2):
        first = even[256 + 8 * m:264 + 8 * m]
        second = odd[256 + 8 * m:264 + 8 * m]
        out_ref[2 * m, start + 16:start + 24, :] = jnp.where(lower, first, pltpu.roll(second, 4, 0))
        out_ref[2 * m + 1, start + 16:start + 24, :] = jnp.where(lower, pltpu.roll(first, 4, 0), second)


def regroup_kernel(in_ref, *out_refs):
    ypos = lax.axis_index("y")
    for e in range(YS):
        for z in range(ZS):
            out_refs[e][z] = in_ref[z, lax.rem(ypos + e, YS)]


def regroup(arrived):
    vmem = pl.BlockSpec(memory_space=pltpu.VMEM)
    return pl.pallas_call(
        regroup_kernel,
        in_specs=[vmem],
        out_specs=[vmem] * YS,
        out_shape=[jax.ShapeDtypeStruct((ZS, 16, LANES), F32)] * YS,
        compiler_params=pltpu.CompilerParams(vmem_limit_bytes=VMEM_ALL),
        name="regroup",
    )(arrived)


def gram_sum_kernel(tiles_ref, *rest):
    in_refs, out_ref, total = rest[:YS], rest[YS], rest[YS + 1]
    ypos = lax.axis_index("y")
    total[...] = jnp.zeros_like(total)
    lane = lax.broadcasted_iota(jnp.int32, (8, LANES), 1)

    def add(z, carry):
        for e in range(YS):
            holder = z * YS + lax.rem(ypos - e + YS, YS)
            for j in range(CAP):
                tile = tiles_ref[j, holder]
                piece = in_refs[e][z, 8 * (j // 2):8 * (j // 2) + 8, :]
                keep = lane < CELLS if j % 2 == 0 else lane >= CELLS
                total[tile] = total[tile] + jnp.where(keep, piece, 0.0)
        return carry

    lax.fori_loop(0, ZS, add, 0)
    groups = N // TX // 2
    for b in range(ROWS // TY):
        for m in range(groups):
            first = total[2 * m * 3 + b]
            second = total[(2 * m + 1) * 3 + b]
            first = first + pltpu.roll(first, CELLS, 1)
            second = second + pltpu.roll(second, CELLS, 1)
            at = (b * groups + m) * 8
            out_ref[at:at + 8, :] = jnp.where(lane < CELLS, first, second)


def gram_sum(arrived, tiles):
    return pl.pallas_call(
        gram_sum_kernel,
        in_specs=[pl.BlockSpec(memory_space=pltpu.SMEM)] + [pl.BlockSpec(memory_space=pltpu.VMEM)] * YS,
        out_specs=pl.BlockSpec(memory_space=pltpu.VMEM),
        out_shape=jax.ShapeDtypeStruct((TILES // 2 * 8, LANES), F32),
        scratch_shapes=[pltpu.VMEM((TILES, 8, LANES), F32)],
        compiler_params=pltpu.CompilerParams(vmem_limit_bytes=VMEM_ALL),
        name="gram_sum",
    )(tiles, *arrived)


def forward_y_kernel(d_ref, s_ref, maps_ref, spread_ref, high_ref, low_ref, out_ref):
    flipped = d_ref[...].reshape(LANES, N).T
    wide = dot(jnp.concatenate(split(flipped), axis=1), spread_ref[...])
    for p in range(2):
        images, turned = [], []
        for r in (2 * p, 2 * p + 1):
            maps = dot(s_ref[r], maps_ref[...])
            real_map, imag_map = maps[:, :LANES], maps[:, LANES:]
            d = wide[:, 2 * r * LANES:(2 * r + 1) * LANES]
            turned_d = wide[:, (2 * r + 1) * LANES:(2 * r + 2) * LANES]
            images.append(real_map * d + imag_map * turned_d)
            turned.append(real_map * turned_d - imag_map * d)
        done = transform(high_ref, low_ref, images, turned)
        store_outgoing(out_ref, 24 * p, done[:, :LANES], done[:, LANES:])


def forward_y(direction, maps, sel_maps, sel_spread, table):
    return pl.pallas_call(
        forward_y_kernel,
        grid=(ROWS // 4,),
        in_specs=[
            pl.BlockSpec((4, 2 * PLANES, N), lambda i: (i, 0, 0)),
            pl.BlockSpec((4, N, LANES), lambda i: (i, 0, 0)),
            whole(sel_maps),
            whole(sel_spread),
            whole(table[0]),
            whole(table[1]),
        ],
        out_specs=pl.BlockSpec((SLABS, 48, LANES), lambda i: (0, i, 0)),
        out_shape=pltpu.HBM((SLABS, 24 * PAIRS, LANES), F32),
        compiler_params=pltpu.CompilerParams(vmem_limit_bytes=VMEM_LIMIT),
        name="forward_y",
    )(*near(direction, maps, sel_maps), *far(sel_spread), *near(*table))


def arrived_rows(ref, index, block):
    parts = []
    for i in range(2):
        start = i * 8 + index if index < 8 else 16 + 4 * i + index - 8
        parts += [ref[pl.ds(start + 24 * p, SLABS, stride=block), :] for p in range(PAIRS)]
    return jnp.concatenate(parts, axis=0)


def middle_kernel(norm_ref, in_ref, *rest):
    g_hbm, tables_hbm = rest[:8], rest[8:12]
    out_ref, table_ref, g_ref, grid_ref, table_sem, g_sem = rest[12:]
    fh_ref, fl_ref, bh_ref, bl_ref = (table_ref.at[i] for i in range(4))
    xpos, core = lax.axis_index("x"), lax.axis_index("core")
    load_tables = [pltpu.make_async_copy(tables_hbm[i], table_ref.at[i], table_sem.at[i]) for i in range(4)]
    load_g = []
    for d in range(4):
        for k in range(2):
            c = 2 * lax.rem(xpos + 4 - d, 4) + lax.rem(core + k, 2)
            load_g.append(pltpu.make_async_copy(g_hbm[4 * k + d], g_ref.at[c], g_sem.at[4 * k + d]))
    for copy in load_tables[:2] + load_g + load_tables[2:]:
        copy.start()
    for copy in load_tables[:2]:
        copy.wait()
    for p in range(PAIRS):
        pieces = [arrived_rows(in_ref, 2 * p + i, BLOCK) for i in range(2)]
        done = transform(fh_ref, fl_ref, pieces, [times_i(x) for x in pieces])
        for i in range(2):
            b = 2 * p + i
            grid_ref[b // TY, pl.ds(b % TY, N, stride=TY), :] = done[:, LANES * i:LANES * (i + 1)]
    for copy in load_g + load_tables[2:]:
        copy.wait()
    left = lax.broadcasted_iota(jnp.int32, (CELLS, LANES), 1) < CELLS
    curve = jnp.zeros((8, LANES), F32)
    groups = N // TX // 2
    for b in range(ROWS // TY):
        for m in range(groups):
            at = (b * groups + m) * 8
            packed = jnp.concatenate([g_ref[c, at:at + 8, :] for c in range(8)], axis=0)
            weights = jnp.concatenate([jnp.where(left, packed, 0.0), jnp.where(left, 0.0, packed)], axis=0)
            cells = slice(2 * m * CELLS, (2 * m + 2) * CELLS)
            tile = grid_ref[b, cells, :]
            w_high, w_low = split(weights)
            t_high, t_low = split(tile)
            applied = dot(jnp.concatenate([w_high, w_low], axis=1), jnp.concatenate([t_high, t_high], axis=0))
            applied = applied + dot(w_high, t_low)
            curve = curve + jnp.sum((tile * applied).reshape(2 * CELLS // 8, 8, LANES), axis=0)
            grid_ref[b, cells, :] = applied
    norm = jnp.broadcast_to(norm_ref[...], (8, LANES)) / (8 * LANES)
    sums = jnp.where(lax.broadcasted_iota(jnp.int32, (8, LANES), 0) == 0, jnp.sum(curve, axis=0, keepdims=True), norm)
    out_ref[:, BLOCK:, :] = jnp.broadcast_to(sums[None], (SLABS, 8, LANES))
    for p in range(PAIRS):
        pieces = [grid_ref[b // TY, pl.ds(b % TY, N, stride=TY), :] for b in (2 * p, 2 * p + 1)]
        done = transform(bh_ref, bl_ref, pieces, [times_i(x) for x in pieces])
        store_outgoing(out_ref, 24 * p, done[:, :LANES], done[:, LANES:])


def middle(norm, arrived, grams, table_in, table_out):
    vmem = pl.BlockSpec(memory_space=pltpu.VMEM)
    hbm = pl.BlockSpec(memory_space=pltpu.HBM)
    return pl.pallas_call(
        middle_kernel,
        in_specs=[vmem] * 2 + [hbm] * 12,
        out_specs=vmem,
        out_shape=near_out(SLABS, BLOCK + 8, LANES),
        scratch_shapes=[
            pltpu.VMEM((4, N, 2 * N), BF16),
            pltpu.VMEM((8, TILES // 2 * 8, LANES), F32),
            pltpu.VMEM((ROWS // TY, N * TY, LANES), F32),
            pltpu.SemaphoreType.DMA((4,)),
            pltpu.SemaphoreType.DMA((8,)),
        ],
        compiler_params=pltpu.CompilerParams(vmem_limit_bytes=VMEM_LIMIT),
        name="middle",
    )(norm, *near(arrived), *far(*grams, *table_in, *table_out))


def backward_y_kernel(in_ref, s_ref, maps_ref, gather_ref, high_ref, low_ref, *rest):
    kept_refs, sent_refs = rest[:2], rest[2:]
    core = lax.axis_index("core")
    block = BLOCK + 8
    curve = jnp.sum(in_ref[pl.ds(BLOCK, SLABS, stride=block), :], axis=0, keepdims=True)
    norm = jnp.sum(in_ref[pl.ds(BLOCK + 1, SLABS, stride=block), :], axis=0, keepdims=True)
    sums = jnp.where(lax.broadcasted_iota(jnp.int32, (8, LANES), 0) == 0, curve, norm)
    sums = jnp.concatenate([sums] + [jnp.zeros_like(sums)] * (N // LANES - 1), axis=1)
    kept_refs[0][QUARTER:, :] = sums
    sent_refs[0][QUARTER:, :] = sums
    for g in range(ROWS // 4):
        highs, lows = [], []
        for p in range(2):
            rows = [4 * g + 2 * p + i for i in range(2)]
            pieces = [arrived_rows(in_ref, r, block) for r in rows]
            done = transform(high_ref, low_ref, pieces, [times_i(x) for x in pieces])
            for i in range(2):
                back = done[:, LANES * i:LANES * (i + 1)]
                maps = dot(s_ref[rows[i]], maps_ref[...])
                high, low = split(maps[:, :LANES] * back - maps[:, LANES:] * times_i(back))
                highs.append(high)
                lows.append(low)
        total = dot(jnp.concatenate(highs + lows, axis=1), gather_ref[...]).T
        for r in range(4):
            a = 4 * g + r
            at = a % (PAIRS // 2) * 2 * PLANES
            quarter = a // (PAIRS // 2) % 2
            rows = total[2 * PLANES * r:2 * PLANES * (r + 1), :]

            @pl.when(core == a // PAIRS)
            def _():
                kept_refs[quarter][at:at + 2 * PLANES, :] = rows

            @pl.when(core != a // PAIRS)
            def _():
                sent_refs[quarter][at:at + 2 * PLANES, :] = rows


def backward_y(arrived, maps, sel_maps, sel_gather, table):
    vmem = pl.BlockSpec(memory_space=pltpu.VMEM)
    quarters = [near_out(QUARTER + 8, N), near_out(QUARTER, N)]
    return pl.pallas_call(
        backward_y_kernel,
        in_specs=[vmem] * 6,
        out_specs=[vmem] * 4,
        out_shape=quarters * 2,
        compiler_params=pltpu.CompilerParams(vmem_limit_bytes=VMEM_LIMIT),
        name="backward_y",
    )(*near(arrived, maps, sel_maps, sel_gather, *table))


def gram_kernel(counts_ref, w_ref, out_ref):
    step = pl.program_id(0)
    owners = w_ref.shape[0]
    at = pl.multiple_of((lax.axis_index("x") * 2 + lax.axis_index("core")) * 8, 8)
    lane = lax.broadcasted_iota(jnp.int32, (8, SB), 1)
    for o in range(owners):
        rows = []
        for j in range(CAP):
            live = counts_ref[j, step * owners + o]
            rows.append(jnp.where(lane < live, w_ref[o, j, pl.ds(at, 8), :], 0.0))
        l_high, l_low = split(jnp.concatenate(rows, axis=0))
        r_high, r_low = split(w_ref[o].reshape(CAP * CELLS, SB))
        gram = dot_nt(jnp.concatenate([l_high, l_low], axis=1), jnp.concatenate([r_high, r_high], axis=1))
        gram = gram + dot_nt(l_high, r_low)
        for m in range(CAP // 2):
            first = gram[16 * m:16 * m + 8, LANES * m:LANES * (m + 1)]
            second = gram[16 * m + 8:16 * m + 16, LANES * m:LANES * (m + 1)]
            out_ref[o, 8 * m:8 * m + 8, :] = jnp.where(lane < CELLS, first, second)


def gram_rows(interp, counts):
    owners = 16
    return pl.pallas_call(
        gram_kernel,
        grid=(SLABS // owners,),
        in_specs=[pl.BlockSpec(memory_space=pltpu.SMEM), pl.BlockSpec((owners, CAP, CELLS, SB), lambda i: (i, 0, 0, 0))],
        out_specs=pl.BlockSpec((owners, 16, LANES), lambda i: (i, 0, 0)),
        out_shape=jax.ShapeDtypeStruct((SLABS, 16, LANES), F32),
        compiler_params=pltpu.CompilerParams(vmem_limit_bytes=VMEM_LIMIT),
        name="gram_rows",
    )(*far(counts, interp))


def share_kernel(a_ref, more_a_ref, b_ref, more_b_ref, residual_ref, out_ref, part_ref, sums_ref):
    first = a_ref[...] + more_a_ref[...]
    curvature = jnp.sum(first[QUARTER:QUARTER + 1, :LANES], axis=1, keepdims=True)
    norm_now = jnp.sum(first[QUARTER + 1:QUARTER + 2, :LANES], axis=1, keepdims=True)
    step = norm_now / curvature
    core = lax.axis_index("core")
    square = jnp.zeros((8, N), F32)
    for i, applied in enumerate((first[:QUARTER], b_ref[...] + more_b_ref[...])):
        rows = pl.ds(i * QUARTER, QUARTER)
        part = residual_ref[core, rows, :] - step * applied
        out_ref[rows, :] = part
        square = square + jnp.sum((part * part).reshape(QUARTER // 8, 8, N), axis=0)
    part = jnp.sum(square[:, :LANES] + square[:, LANES:2 * LANES] + square[:, 2 * LANES:], axis=0, keepdims=True)
    part_ref[...] = jnp.broadcast_to(part[None], part_ref.shape)
    sums_ref[...] = jnp.where(lax.broadcasted_iota(jnp.int32, (8, LANES), 0) == 0, step, norm_now)


def residual_share(first, second, residual):
    vmem = pl.BlockSpec(memory_space=pltpu.VMEM)
    return pl.pallas_call(
        share_kernel,
        in_specs=[vmem] * 5,
        out_specs=[vmem] * 3,
        out_shape=[
            near_out(HALF_ROWS, N),
            near_out(2 * SLABS, 1, LANES),
            near_out(8, LANES),
        ],
        compiler_params=pltpu.CompilerParams(vmem_limit_bytes=VMEM_LIMIT),
        name="residual_share",
    )(*near(*first, *second, residual))


def image_kernel(sums_ref, image_ref, direction_ref, out_ref):
    out_ref[...] = image_ref[...] + sums_ref[0:1, 0:1] * direction_ref[...]


def image_update(sums, image, direction):
    vmem = pl.BlockSpec(memory_space=pltpu.VMEM)
    return pl.pallas_call(
        image_kernel,
        in_specs=[vmem] * 3,
        out_specs=vmem,
        out_shape=jax.ShapeDtypeStruct(image.shape, F32),
        name="image_update",
    )(*near(sums, image, direction))


def finish_kernel(sums_ref, parts_ref, direction_ref, own_ref, other_ref, residual_ref, next_ref):
    ratio = jnp.sum(jnp.sum(parts_ref[...], axis=0), axis=1, keepdims=True) / sums_ref[1:2, 0:1]
    core = lax.axis_index("core")
    for half, ref in ((core, own_ref), (1 - core, other_ref)):
        residual_ref[half] = ref[...]
        next_ref[half] = ref[...] + ratio * direction_ref[half]


def finish(sums, parts, direction, own, other):
    vmem = pl.BlockSpec(memory_space=pltpu.VMEM)
    full = jax.ShapeDtypeStruct(direction.shape, F32)
    return pl.pallas_call(
        finish_kernel,
        in_specs=[vmem] * 5,
        out_specs=[vmem, vmem],
        out_shape=[full, full],
        compiler_params=pltpu.CompilerParams(vmem_limit_bytes=VMEM_LIMIT),
        name="finish",
    )(*near(sums, parts, direction, own, other))


def swap_core(value):
    return lax.ppermute(value, "core", [(0, 1), (1, 0)])


def to_next(values, axis, count):
    return list(values[:1]) + [
        lax.ppermute(values[d], axis, [(i, (i + d) % count) for i in range(count)]) for d in range(1, count)
    ]


def swap_x(value, mask):
    return lax.ppermute(value, "x", [(i, i ^ mask) for i in range(4)])


def from_x(value):
    return [lax.ppermute(value, "x", [(i, (i + d) % 4) for i in range(4)]) for d in range(1, 4)]


def body(image_x, residual, direction, sensitivity, interp, slot_tile, counts):
    sending, arrival = ([tuple(jnp.asarray(t) for t in pair) for pair in pairs] for pairs in dft_tables())
    sel_maps, sel_spread, sel_gather = (jnp.asarray(t) for t in selections())
    image_t, residual_t, direction_t = (jnp.transpose(a, (0, 2, 1)) for a in (image_x, residual, direction))

    grams = gram_rows(interp[0], counts[0].T)
    grams = lax.all_to_all(grams.reshape(ZS, YS, 16, LANES), "z", split_axis=0, concat_axis=0, tiled=True)
    outgoing = forward_y(direction_t, sensitivity, sel_maps, sel_spread, sending[0])
    outgoing, grams = lax.optimization_barrier((outgoing, grams))
    grams = regroup(grams)
    grams = gram_sum(to_next(grams, "y", YS), slot_tile[0].T)
    grams = [grams] + from_x(grams)
    grams = grams + [swap_core(g) for g in grams]

    pencils = lax.all_to_all(outgoing, SLAB, split_axis=0, concat_axis=0, tiled=True)
    norm = jnp.sum(residual_t * residual_t).reshape(1, 1)
    outgoing = middle(norm, pencils.reshape(-1, LANES), grams, arrival[0], sending[1])
    slab_rows = lax.all_to_all(outgoing, SLAB, split_axis=0, concat_axis=0, tiled=True)
    kept_a, kept_b, sent_a, sent_b = backward_y(
        slab_rows.reshape(-1, LANES), sensitivity, sel_maps, sel_gather, arrival[1]
    )

    kept_a = kept_a + swap_core(sent_a)
    kept_b = kept_b + swap_core(sent_b)
    kept_a = kept_a + swap_x(kept_a, 1)
    kept_b = kept_b + swap_x(kept_b, 3)
    halves = (2, HALF_ROWS, N)
    half, parts, sums = residual_share(
        (kept_a, swap_x(kept_a, 3)), (kept_b, swap_x(kept_b, 1)), residual_t.reshape(halves)
    )
    parts = lax.all_to_all(parts, SLAB + ("core",), split_axis=0, concat_axis=0, tiled=True)
    next_image = image_update(sums, image_t.reshape(halves), direction_t.reshape(halves))
    next_residual, next_direction = finish(sums, parts, direction_t.reshape(halves), half, swap_core(half))
    return tuple(
        jnp.transpose(a.reshape(direction_t.shape), (0, 2, 1)) for a in (next_image, next_residual, next_direction)
    )


def solution(mesh):
    fine = Mesh(mesh.devices.reshape(8, 4, 4, 2), ALL)
    rows = P(SLAB, None, None)
    return jax.shard_map(
        body,
        mesh=fine,
        in_specs=(
            rows,
            rows,
            rows,
            P(SLAB, None, COIL),
            P(SLAB, None, None, None, None),
            rows,
            rows,
        ),
        out_specs=(rows, rows, rows),
        check_vma=False,
    )
```

```python
import jax
import jax.numpy as jnp
import ml_dtypes
import numpy as np
from jax import lax
from jax.experimental import pallas as pl
from jax.experimental.pallas import tpu as pltpu
from jax.sharding import Mesh
from jax.sharding import PartitionSpec as P

N = 384
SLABS = 32
ROWS = 12
PAIRS = ROWS // 2
LANES = 128
PLANES = 16
TX = 16
TY = 4
CELLS = TX * TY
TILES = 72
CAP = 4
SB = 128
SLAB = ("z", "y")
COIL = ("x", "core")
ALL = ("z", "y", "x", "core")
HALF_ROWS = PAIRS * 2 * PLANES
ZS = 8
YS = 4
QUARTER = HALF_ROWS // 2
BLOCK = 24 * PAIRS
HALF = LANES // 2
COILS = HALF // PLANES
VMEM_LIMIT = 32 * 1024 * 1024
VMEM_ALL = 56 * 1024 * 1024
F32 = jnp.float32
BF16 = jnp.bfloat16
NT = (((1,), (1,)), ((), ()))


def split_table(table):
    table = table.astype(np.float32)
    high = table.astype(ml_dtypes.bfloat16)
    low = (table - high.astype(np.float32)).astype(ml_dtypes.bfloat16)
    return high, low


def dft_tables():
    pos = np.arange(N)
    phase = (pos[:, None] * pos[None, :] % N) * (2.0 * np.pi / N)
    real = np.cos(phase) / np.sqrt(N)
    imag = -np.sin(phase) / np.sqrt(N)
    base = ROWS * np.arange(SLABS)[:, None]
    rows = np.concatenate([(base + np.arange(8)).reshape(-1), (base + np.arange(8, ROWS)).reshape(-1)])
    cols = np.concatenate([base.reshape(-1) + 2 * p + i for i in range(2) for p in range(PAIRS)])
    sending = [split_table(np.concatenate([real[rows], sign * imag[rows]], axis=1)) for sign in (1, -1)]
    arrival = [split_table(np.concatenate([real[:, cols], sign * imag[:, cols]], axis=1)) for sign in (1, -1)]
    return sending, arrival


def selections():
    place = np.arange(LANES)
    part, coil, plane = place // HALF, place // PLANES % COILS, place % PLANES
    group, src_part, src_plane = place // (2 * PLANES), place // PLANES % 2, place % PLANES
    same = (group[:, None] == coil) & (src_plane[:, None] == plane)
    maps = np.concatenate([same & (src_part[:, None] == 0), same & (src_part[:, None] == 1)], axis=1)
    spread, gather = [], []
    for r in range(4):
        hit = (group[:, None] == r) & (src_plane[:, None] == plane)
        from_real = hit & (src_part[:, None] == 0)
        from_imag = hit & (src_part[:, None] == 1)
        spread.append((from_real & (part == 0)) + (from_imag & (part == 1)) + 0.0)
        spread.append((from_real & (part == 1)) + 0.0 - (from_imag & (part == 0)))
        gather.append((group == r) & (src_plane == plane[:, None]) & (src_part == part[:, None]))
    spread = np.concatenate([np.concatenate(spread, axis=1)] * 2, axis=0)
    gather = np.concatenate(gather * 2, axis=0)
    return tuple(a.astype(ml_dtypes.bfloat16) for a in (maps, spread, gather))


def split(value):
    high = value.astype(BF16)
    return high, (value - high.astype(F32)).astype(BF16)


def dot(a, b):
    return jnp.dot(a, b, preferred_element_type=F32)


def dot_nt(a, b):
    return lax.dot_general(a, b, NT, preferred_element_type=F32)


def near(*arrays):
    return [pltpu.with_memory_space_constraint(a, pltpu.VMEM) for a in arrays]


def far(*arrays):
    return [pltpu.with_memory_space_constraint(a, pltpu.HBM) for a in arrays]


def near_out(*shape):
    return pltpu.VMEM(shape, F32)


def whole(array):
    return pl.BlockSpec(array.shape, lambda i: (0,) * array.ndim)


def times_i(value):
    rolled = pltpu.roll(value, HALF, 1)
    return jnp.where(lax.broadcasted_iota(jnp.int32, value.shape, 1) < HALF, -rolled, rolled)


def transform(high_ref, low_ref, pieces, turned):
    highs, lows = [], []
    for piece, turn in zip(pieces, turned):
        piece_high, piece_low = split(piece)
        turn_high, turn_low = (times_i(piece_high), times_i(piece_low)) if turn is None else split(turn)
        highs.append(jnp.concatenate([piece_high, turn_high], axis=0))
        lows.append(jnp.concatenate([piece_low, turn_low], axis=0))
    high = jnp.concatenate(highs, axis=1)
    low = jnp.concatenate(lows, axis=1)
    return dot(high_ref[...], high) + (dot(high_ref[...], low) + dot(low_ref[...], high))


def store_outgoing(out_ref, start, even, odd):
    out_ref[:, start:start + 8, :] = even[:256].reshape(SLABS, 8, LANES)
    out_ref[:, start + 8:start + 16, :] = odd[:256].reshape(SLABS, 8, LANES)
    lower = lax.broadcasted_iota(jnp.int32, (8, LANES), 0) < 4
    for m in range(SLABS // 2):
        first = even[256 + 8 * m:264 + 8 * m]
        second = odd[256 + 8 * m:264 + 8 * m]
        out_ref[2 * m, start + 16:start + 24, :] = jnp.where(lower, first, pltpu.roll(second, 4, 0))
        out_ref[2 * m + 1, start + 16:start + 24, :] = jnp.where(lower, pltpu.roll(first, 4, 0), second)


def regroup_kernel(in_ref, *out_refs):
    ypos = lax.axis_index("y")
    for e in range(YS):
        for z in range(ZS):
            out_refs[e][z] = in_ref[z, lax.rem(ypos + e, YS)]


def regroup(arrived):
    vmem = pl.BlockSpec(memory_space=pltpu.VMEM)
    return pl.pallas_call(
        regroup_kernel,
        in_specs=[vmem],
        out_specs=[vmem] * YS,
        out_shape=[jax.ShapeDtypeStruct((ZS, 16, LANES), F32)] * YS,
        compiler_params=pltpu.CompilerParams(vmem_limit_bytes=VMEM_ALL),
        name="regroup",
    )(arrived)


def gram_sum_kernel(tiles_ref, *rest):
    in_refs, out_ref, total = rest[:YS], rest[YS], rest[YS + 1]
    ypos = lax.axis_index("y")
    total[...] = jnp.zeros_like(total)
    lane = lax.broadcasted_iota(jnp.int32, (8, LANES), 1)

    def add(z, carry):
        for e in range(YS):
            holder = z * YS + lax.rem(ypos - e + YS, YS)
            for j in range(CAP):
                tile = tiles_ref[j, holder]
                piece = in_refs[e][z, 8 * (j // 2):8 * (j // 2) + 8, :]
                keep = lane < CELLS if j % 2 == 0 else lane >= CELLS
                total[tile] = total[tile] + jnp.where(keep, piece, 0.0)
        return carry

    lax.fori_loop(0, ZS, add, 0)
    groups = N // TX // 2
    for b in range(ROWS // TY):
        for m in range(groups):
            first = total[2 * m * 3 + b]
            second = total[(2 * m + 1) * 3 + b]
            first = first + pltpu.roll(first, CELLS, 1)
            second = second + pltpu.roll(second, CELLS, 1)
            at = (b * groups + m) * 8
            out_ref[at:at + 8, :] = jnp.where(lane < CELLS, first, second)


def gram_sum(arrived, tiles):
    return pl.pallas_call(
        gram_sum_kernel,
        in_specs=[pl.BlockSpec(memory_space=pltpu.SMEM)] + [pl.BlockSpec(memory_space=pltpu.VMEM)] * YS,
        out_specs=pl.BlockSpec(memory_space=pltpu.VMEM),
        out_shape=jax.ShapeDtypeStruct((TILES // 2 * 8, LANES), F32),
        scratch_shapes=[pltpu.VMEM((TILES, 8, LANES), F32)],
        compiler_params=pltpu.CompilerParams(vmem_limit_bytes=VMEM_ALL),
        name="gram_sum",
    )(tiles, *arrived)


def forward_y_kernel(d_ref, s_ref, maps_ref, spread_ref, high_ref, low_ref, out_ref):
    flipped = d_ref[...].reshape(LANES, N).T
    wide = dot(jnp.concatenate(split(flipped), axis=1), spread_ref[...])
    for p in range(2):
        images, turned = [], []
        for r in (2 * p, 2 * p + 1):
            maps = dot(s_ref[r], maps_ref[...])
            real_map, imag_map = maps[:, :LANES], maps[:, LANES:]
            d = wide[:, 2 * r * LANES:(2 * r + 1) * LANES]
            turned_d = wide[:, (2 * r + 1) * LANES:(2 * r + 2) * LANES]
            images.append(real_map * d + imag_map * turned_d)
            turned.append(real_map * turned_d - imag_map * d)
        done = transform(high_ref, low_ref, images, turned)
        store_outgoing(out_ref, 24 * p, done[:, :LANES], done[:, LANES:])


def forward_y(direction, maps, sel_maps, sel_spread, table):
    return pl.pallas_call(
        forward_y_kernel,
        grid=(ROWS // 4,),
        in_specs=[
            pl.BlockSpec((4, 2 * PLANES, N), lambda i: (i, 0, 0)),
            pl.BlockSpec((4, N, LANES), lambda i: (i, 0, 0)),
            whole(sel_maps),
            whole(sel_spread),
            whole(table[0]),
            whole(table[1]),
        ],
        out_specs=pl.BlockSpec((SLABS, 48, LANES), lambda i: (0, i, 0)),
        out_shape=pltpu.HBM((SLABS, 24 * PAIRS, LANES), F32),
        compiler_params=pltpu.CompilerParams(vmem_limit_bytes=VMEM_LIMIT),
        name="forward_y",
    )(*near(direction, maps, sel_maps), *far(sel_spread), *near(*table))


def arrived_rows(ref, index, block):
    parts = []
    for i in range(2):
        start = i * 8 + index if index < 8 else 16 + 4 * i + index - 8
        parts += [ref[pl.ds(start + 24 * p, SLABS, stride=block), :] for p in range(PAIRS)]
    return jnp.concatenate(parts, axis=0)


def middle_kernel(norm_ref, in_ref, *rest):
    g_hbm, tables_hbm = rest[:8], rest[8:12]
    out_ref, table_ref, g_ref, grid_ref, table_sem, g_sem = rest[12:]
    fh_ref, fl_ref, bh_ref, bl_ref = (table_ref.at[i] for i in range(4))
    xpos, core = lax.axis_index("x"), lax.axis_index("core")
    load_tables = [pltpu.make_async_copy(tables_hbm[i], table_ref.at[i], table_sem.at[i]) for i in range(4)]
    load_g = []
    for d in range(4):
        for k in range(2):
            c = 2 * lax.rem(xpos + 4 - d, 4) + lax.rem(core + k, 2)
            load_g.append(pltpu.make_async_copy(g_hbm[4 * k + d], g_ref.at[c], g_sem.at[4 * k + d]))
    for copy in load_tables[:2] + load_g + load_tables[2:]:
        copy.start()
    for p in range(PAIRS):
        pieces = [arrived_rows(in_ref, 2 * p + i, BLOCK) for i in range(2)]
        if p == 0:
            for copy in load_tables[:2]:
                copy.wait()
        done = transform(fh_ref, fl_ref, pieces, [None, None])
        for i in range(2):
            b = 2 * p + i
            grid_ref[b // TY, pl.ds(b % TY, N, stride=TY), :] = done[:, LANES * i:LANES * (i + 1)]
    for copy in load_g + load_tables[2:]:
        copy.wait()
    left = lax.broadcasted_iota(jnp.int32, (CELLS, LANES), 1) < CELLS
    curve = jnp.zeros((8, LANES), F32)
    groups = N // TX // 2
    for b in range(ROWS // TY):
        for m in range(groups):
            at = (b * groups + m) * 8
            packed = jnp.concatenate([g_ref[c, at:at + 8, :] for c in range(8)], axis=0)
            weights = jnp.concatenate([jnp.where(left, packed, 0.0), jnp.where(left, 0.0, packed)], axis=0)
            cells = slice(2 * m * CELLS, (2 * m + 2) * CELLS)
            tile = grid_ref[b, cells, :]
            w_high, w_low = split(weights)
            t_high, t_low = split(tile)
            applied = dot(jnp.concatenate([w_high, w_low], axis=1), jnp.concatenate([t_high, t_high], axis=0))
            applied = applied + dot(w_high, t_low)
            curve = curve + jnp.sum((tile * applied).reshape(2 * CELLS // 8, 8, LANES), axis=0)
            grid_ref[b, cells, :] = applied
    norm = jnp.broadcast_to(norm_ref[...], (8, LANES)) / (8 * LANES)
    sums = jnp.where(lax.broadcasted_iota(jnp.int32, (8, LANES), 0) == 0, jnp.sum(curve, axis=0, keepdims=True), norm)
    out_ref[:, BLOCK:, :] = jnp.broadcast_to(sums[None], (SLABS, 8, LANES))
    for p in range(PAIRS):
        pieces = [grid_ref[b // TY, pl.ds(b % TY, N, stride=TY), :] for b in (2 * p, 2 * p + 1)]
        done = transform(bh_ref, bl_ref, pieces, [None, None])
        store_outgoing(out_ref, 24 * p, done[:, :LANES], done[:, LANES:])


def middle(norm, arrived, grams, table_in, table_out):
    vmem = pl.BlockSpec(memory_space=pltpu.VMEM)
    hbm = pl.BlockSpec(memory_space=pltpu.HBM)
    return pl.pallas_call(
        middle_kernel,
        in_specs=[vmem] * 2 + [hbm] * 12,
        out_specs=vmem,
        out_shape=near_out(SLABS, BLOCK + 8, LANES),
        scratch_shapes=[
            pltpu.VMEM((4, N, 2 * N), BF16),
            pltpu.VMEM((8, TILES // 2 * 8, LANES), F32),
            pltpu.VMEM((ROWS // TY, N * TY, LANES), F32),
            pltpu.SemaphoreType.DMA((4,)),
            pltpu.SemaphoreType.DMA((8,)),
        ],
        compiler_params=pltpu.CompilerParams(vmem_limit_bytes=VMEM_LIMIT),
        name="middle",
    )(norm, *near(arrived), *far(*grams, *table_in, *table_out))


def backward_y_kernel(in_ref, s_ref, maps_ref, gather_ref, high_ref, low_ref, *rest):
    kept_refs, sent_refs = rest[:2], rest[2:]
    core = lax.axis_index("core")
    block = BLOCK + 8
    curve = jnp.sum(in_ref[pl.ds(BLOCK, SLABS, stride=block), :], axis=0, keepdims=True)
    norm = jnp.sum(in_ref[pl.ds(BLOCK + 1, SLABS, stride=block), :], axis=0, keepdims=True)
    sums = jnp.where(lax.broadcasted_iota(jnp.int32, (8, LANES), 0) == 0, curve, norm)
    sums = jnp.concatenate([sums] + [jnp.zeros_like(sums)] * (N // LANES - 1), axis=1)
    kept_refs[0][QUARTER:, :] = sums
    sent_refs[0][QUARTER:, :] = sums
    for g in range(ROWS // 4):
        highs, lows = [], []
        for p in range(2):
            rows = [4 * g + 2 * p + i for i in range(2)]
            pieces = [arrived_rows(in_ref, r, block) for r in rows]
            done = transform(high_ref, low_ref, pieces, [None, None])
            for i in range(2):
                back = done[:, LANES * i:LANES * (i + 1)]
                maps = dot(s_ref[rows[i]], maps_ref[...])
                high, low = split(maps[:, :LANES] * back - maps[:, LANES:] * times_i(back))
                highs.append(high)
                lows.append(low)
        total = dot(jnp.concatenate(highs + lows, axis=1), gather_ref[...]).T
        for r in range(4):
            a = 4 * g + r
            at = a % (PAIRS // 2) * 2 * PLANES
            quarter = a // (PAIRS // 2) % 2
            rows = total[2 * PLANES * r:2 * PLANES * (r + 1), :]

            @pl.when(core == a // PAIRS)
            def _():
                kept_refs[quarter][at:at + 2 * PLANES, :] = rows

            @pl.when(core != a // PAIRS)
            def _():
                sent_refs[quarter][at:at + 2 * PLANES, :] = rows


def backward_y(arrived, maps, sel_maps, sel_gather, table):
    vmem = pl.BlockSpec(memory_space=pltpu.VMEM)
    quarters = [near_out(QUARTER + 8, N), near_out(QUARTER, N)]
    return pl.pallas_call(
        backward_y_kernel,
        in_specs=[vmem] * 6,
        out_specs=[vmem] * 4,
        out_shape=quarters * 2,
        compiler_params=pltpu.CompilerParams(vmem_limit_bytes=VMEM_LIMIT),
        name="backward_y",
    )(*near(arrived, maps, sel_maps, sel_gather, *table))


def gram_kernel(counts_ref, w_ref, out_ref):
    step = pl.program_id(0)
    owners = w_ref.shape[0]
    at = pl.multiple_of((lax.axis_index("x") * 2 + lax.axis_index("core")) * 8, 8)
    lane = lax.broadcasted_iota(jnp.int32, (8, SB), 1)
    for o in range(owners):
        rows = []
        for j in range(CAP):
            live = counts_ref[j, step * owners + o]
            rows.append(jnp.where(lane < live, w_ref[o, j, pl.ds(at, 8), :], 0.0))
        l_high, l_low = split(jnp.concatenate(rows, axis=0))
        r_high, r_low = split(w_ref[o].reshape(CAP * CELLS, SB))
        both = dot_nt(jnp.concatenate([l_high, l_low], axis=0), r_high)
        gram = both[:CAP * 8] + (both[CAP * 8:] + dot_nt(l_high, r_low))
        for m in range(CAP // 2):
            first = gram[16 * m:16 * m + 8, LANES * m:LANES * (m + 1)]
            second = gram[16 * m + 8:16 * m + 16, LANES * m:LANES * (m + 1)]
            out_ref[o, 8 * m:8 * m + 8, :] = jnp.where(lane < CELLS, first, second)


def gram_rows(interp, counts):
    owners = 16
    return pl.pallas_call(
        gram_kernel,
        grid=(SLABS // owners,),
        in_specs=[pl.BlockSpec(memory_space=pltpu.SMEM), pl.BlockSpec((owners, CAP, CELLS, SB), lambda i: (i, 0, 0, 0))],
        out_specs=pl.BlockSpec((owners, 16, LANES), lambda i: (i, 0, 0)),
        out_shape=jax.ShapeDtypeStruct((SLABS, 16, LANES), F32),
        compiler_params=pltpu.CompilerParams(vmem_limit_bytes=VMEM_LIMIT),
        name="gram_rows",
    )(*far(counts, interp))


def share_kernel(a_ref, more_a_ref, b_ref, more_b_ref, residual_ref, out_ref, part_ref, sums_ref):
    first = a_ref[...] + more_a_ref[...]
    curvature = jnp.sum(first[QUARTER:QUARTER + 1, :LANES], axis=1, keepdims=True)
    norm_now = jnp.sum(first[QUARTER + 1:QUARTER + 2, :LANES], axis=1, keepdims=True)
    step = norm_now / curvature
    core = lax.axis_index("core")
    square = jnp.zeros((8, N), F32)
    for i, applied in enumerate((first[:QUARTER], b_ref[...] + more_b_ref[...])):
        rows = pl.ds(i * QUARTER, QUARTER)
        part = residual_ref[core, rows, :] - step * applied
        out_ref[rows, :] = part
        square = square + jnp.sum((part * part).reshape(QUARTER // 8, 8, N), axis=0)
    part = jnp.sum(square[:, :LANES] + square[:, LANES:2 * LANES] + square[:, 2 * LANES:], axis=0, keepdims=True)
    part_ref[...] = jnp.broadcast_to(part[None], part_ref.shape)
    sums_ref[...] = jnp.where(lax.broadcasted_iota(jnp.int32, (8, LANES), 0) == 0, step, norm_now)


def residual_share(first, second, residual):
    vmem = pl.BlockSpec(memory_space=pltpu.VMEM)
    return pl.pallas_call(
        share_kernel,
        in_specs=[vmem] * 5,
        out_specs=[vmem] * 3,
        out_shape=[
            near_out(HALF_ROWS, N),
            near_out(2 * SLABS, 1, LANES),
            near_out(8, LANES),
        ],
        compiler_params=pltpu.CompilerParams(vmem_limit_bytes=VMEM_LIMIT),
        name="residual_share",
    )(*near(*first, *second, residual))


def image_kernel(sums_ref, image_ref, direction_ref, out_ref):
    out_ref[...] = image_ref[...] + sums_ref[0:1, 0:1] * direction_ref[...]


def image_update(sums, image, direction):
    vmem = pl.BlockSpec(memory_space=pltpu.VMEM)
    return pl.pallas_call(
        image_kernel,
        in_specs=[vmem] * 3,
        out_specs=vmem,
        out_shape=jax.ShapeDtypeStruct(image.shape, F32),
        name="image_update",
    )(*near(sums, image, direction))


def finish_kernel(sums_ref, parts_ref, direction_ref, own_ref, other_ref, residual_ref, next_ref):
    ratio = jnp.sum(jnp.sum(parts_ref[...], axis=0), axis=1, keepdims=True) / sums_ref[1:2, 0:1]
    core = lax.axis_index("core")
    for half, ref in ((core, own_ref), (1 - core, other_ref)):
        residual_ref[half] = ref[...]
        next_ref[half] = ref[...] + ratio * direction_ref[half]


def finish(sums, parts, direction, own, other):
    vmem = pl.BlockSpec(memory_space=pltpu.VMEM)
    full = jax.ShapeDtypeStruct(direction.shape, F32)
    return pl.pallas_call(
        finish_kernel,
        in_specs=[vmem] * 5,
        out_specs=[vmem, vmem],
        out_shape=[full, full],
        compiler_params=pltpu.CompilerParams(vmem_limit_bytes=VMEM_LIMIT),
        name="finish",
    )(*near(sums, parts, direction, own, other))


def swap_core(value):
    return lax.ppermute(value, "core", [(0, 1), (1, 0)])


def to_next(values, axis, count):
    return list(values[:1]) + [
        lax.ppermute(values[d], axis, [(i, (i + d) % count) for i in range(count)]) for d in range(1, count)
    ]


def swap_x(value, mask):
    return lax.ppermute(value, "x", [(i, i ^ mask) for i in range(4)])


def from_x(value):
    return [lax.ppermute(value, "x", [(i, (i + d) % 4) for i in range(4)]) for d in range(1, 4)]


def body(image_x, residual, direction, sensitivity, interp, slot_tile, counts):
    sending, arrival = ([tuple(jnp.asarray(t) for t in pair) for pair in pairs] for pairs in dft_tables())
    sel_maps, sel_spread, sel_gather = (jnp.asarray(t) for t in selections())
    image_t, residual_t, direction_t = (jnp.transpose(a, (0, 2, 1)) for a in (image_x, residual, direction))

    grams = gram_rows(interp[0], counts[0].T)
    grams = lax.all_to_all(grams.reshape(ZS, YS, 16, LANES), "z", split_axis=0, concat_axis=0, tiled=True)
    outgoing = forward_y(direction_t, sensitivity, sel_maps, sel_spread, sending[0])
    outgoing, grams = lax.optimization_barrier((outgoing, grams))
    grams = regroup(grams)
    grams = gram_sum(to_next(grams, "y", YS), slot_tile[0].T)
    grams = [grams] + from_x(grams)
    grams = grams + [swap_core(g) for g in grams]

    pencils = lax.all_to_all(outgoing, SLAB, split_axis=0, concat_axis=0, tiled=True)
    norm = jnp.sum(residual_t * residual_t).reshape(1, 1)
    outgoing = middle(norm, pencils.reshape(-1, LANES), grams, arrival[0], sending[1])
    slab_rows = lax.all_to_all(outgoing, SLAB, split_axis=0, concat_axis=0, tiled=True)
    kept_a, kept_b, sent_a, sent_b = backward_y(
        slab_rows.reshape(-1, LANES), sensitivity, sel_maps, sel_gather, arrival[1]
    )

    kept_a = kept_a + swap_core(sent_a)
    kept_b = kept_b + swap_core(sent_b)
    kept_a = kept_a + swap_x(kept_a, 1)
    kept_b = kept_b + swap_x(kept_b, 3)
    halves = (2, HALF_ROWS, N)
    half, parts, sums = residual_share(
        (kept_a, swap_x(kept_a, 3)), (kept_b, swap_x(kept_b, 1)), residual_t.reshape(halves)
    )
    parts = lax.all_to_all(parts, SLAB + ("core",), split_axis=0, concat_axis=0, tiled=True)
    next_image = image_update(sums, image_t.reshape(halves), direction_t.reshape(halves))
    next_residual, next_direction = finish(sums, parts, direction_t.reshape(halves), half, swap_core(half))
    return tuple(
        jnp.transpose(a.reshape(direction_t.shape), (0, 2, 1)) for a in (next_image, next_residual, next_direction)
    )


def solution(mesh):
    fine = Mesh(mesh.devices.reshape(8, 4, 4, 2), ALL)
    rows = P(SLAB, None, None)
    return jax.shard_map(
        body,
        mesh=fine,
        in_specs=(
            rows,
            rows,
            rows,
            P(SLAB, None, COIL),
            P(SLAB, None, None, None, None),
            rows,
            rows,
        ),
        out_specs=(rows, rows, rows),
        check_vma=False,
    )
```

```python
import jax
import jax.numpy as jnp
import ml_dtypes
import numpy as np
from jax import lax
from jax.experimental import pallas as pl
from jax.experimental.pallas import tpu as pltpu
from jax.sharding import Mesh
from jax.sharding import PartitionSpec as P

N = 384
SLABS = 32
ROWS = 12
PAIRS = ROWS // 2
LANES = 128
PLANES = 16
TX = 16
TY = 4
CELLS = TX * TY
TILES = 72
CAP = 4
SB = 128
SLAB = ("z", "y")
COIL = ("x", "core")
ALL = ("z", "y", "x", "core")
HALF_ROWS = PAIRS * 2 * PLANES
ZS = 8
YS = 4
QUARTER = HALF_ROWS // 2
BLOCK = 24 * PAIRS
HALF = LANES // 2
COILS = HALF // PLANES
VMEM_LIMIT = 32 * 1024 * 1024
VMEM_ALL = 56 * 1024 * 1024
F32 = jnp.float32
BF16 = jnp.bfloat16
NT = (((1,), (1,)), ((), ()))


def split_table(table):
    table = table.astype(np.float32)
    high = table.astype(ml_dtypes.bfloat16)
    low = (table - high.astype(np.float32)).astype(ml_dtypes.bfloat16)
    return high, low


def dft_tables():
    pos = np.arange(N)
    phase = (pos[:, None] * pos[None, :] % N) * (2.0 * np.pi / N)
    real = np.cos(phase) / np.sqrt(N)
    imag = -np.sin(phase) / np.sqrt(N)
    base = ROWS * np.arange(SLABS)[:, None]
    rows = np.concatenate([(base + np.arange(8)).reshape(-1), (base + np.arange(8, ROWS)).reshape(-1)])
    cols = np.concatenate([base.reshape(-1) + 2 * p + i for i in range(2) for p in range(PAIRS)])
    sending = [split_table(np.concatenate([real[rows], sign * imag[rows]], axis=1)) for sign in (1, -1)]
    arrival = [split_table(np.concatenate([real[:, cols], sign * imag[:, cols]], axis=1)) for sign in (1, -1)]
    return sending, arrival


def selections():
    place = np.arange(LANES)
    part, coil, plane = place // HALF, place // PLANES % COILS, place % PLANES
    group, src_part, src_plane = place // (2 * PLANES), place // PLANES % 2, place % PLANES
    same = (group[:, None] == coil) & (src_plane[:, None] == plane)
    maps = np.concatenate([same & (src_part[:, None] == 0), same & (src_part[:, None] == 1)], axis=1)
    spread, gather = [], []
    for r in range(4):
        hit = (group[:, None] == r) & (src_plane[:, None] == plane)
        from_real = hit & (src_part[:, None] == 0)
        from_imag = hit & (src_part[:, None] == 1)
        spread.append((from_real & (part == 0)) + (from_imag & (part == 1)) + 0.0)
        spread.append((from_real & (part == 1)) + 0.0 - (from_imag & (part == 0)))
        gather.append((group == r) & (src_plane == plane[:, None]) & (src_part == part[:, None]))
    spread = np.concatenate([np.concatenate(spread, axis=1)] * 2, axis=0)
    gather = np.concatenate(gather * 2, axis=0)
    return tuple(a.astype(ml_dtypes.bfloat16) for a in (maps, spread, gather))


def split(value):
    high = value.astype(BF16)
    return high, (value - high.astype(F32)).astype(BF16)


def dot(a, b):
    return jnp.dot(a, b, preferred_element_type=F32)


def dot_nt(a, b):
    return lax.dot_general(a, b, NT, preferred_element_type=F32)


def near(*arrays):
    return [pltpu.with_memory_space_constraint(a, pltpu.VMEM) for a in arrays]


def far(*arrays):
    return [pltpu.with_memory_space_constraint(a, pltpu.HBM) for a in arrays]


def near_out(*shape):
    return pltpu.VMEM(shape, F32)


def times_i(value):
    rolled = pltpu.roll(value, HALF, 1)
    return jnp.where(lax.broadcasted_iota(jnp.int32, value.shape, 1) < HALF, -rolled, rolled)


def transform(high_ref, low_ref, pieces, turned):
    highs, lows = [], []
    for piece, turn in zip(pieces, turned):
        piece_high, piece_low = split(piece)
        turn_high, turn_low = (times_i(piece_high), times_i(piece_low)) if turn is None else split(turn)
        highs.append(jnp.concatenate([piece_high, turn_high], axis=0))
        lows.append(jnp.concatenate([piece_low, turn_low], axis=0))
    high = jnp.concatenate(highs, axis=1)
    low = jnp.concatenate(lows, axis=1)
    return dot(high_ref[...], high) + (dot(high_ref[...], low) + dot(low_ref[...], high))


def store_outgoing(out_ref, start, even, odd):
    out_ref[:, start:start + 8, :] = even[:256].reshape(SLABS, 8, LANES)
    out_ref[:, start + 8:start + 16, :] = odd[:256].reshape(SLABS, 8, LANES)
    lower = lax.broadcasted_iota(jnp.int32, (8, LANES), 0) < 4
    for m in range(SLABS // 2):
        first = even[256 + 8 * m:264 + 8 * m]
        second = odd[256 + 8 * m:264 + 8 * m]
        out_ref[2 * m, start + 16:start + 24, :] = jnp.where(lower, first, pltpu.roll(second, 4, 0))
        out_ref[2 * m + 1, start + 16:start + 24, :] = jnp.where(lower, pltpu.roll(first, 4, 0), second)


def regroup_kernel(in_ref, *out_refs):
    ypos = lax.axis_index("y")
    for e in range(YS):
        for z in range(ZS):
            out_refs[e][z] = in_ref[z, lax.rem(ypos + e, YS)]


def regroup(arrived):
    vmem = pl.BlockSpec(memory_space=pltpu.VMEM)
    return pl.pallas_call(
        regroup_kernel,
        in_specs=[vmem],
        out_specs=[vmem] * YS,
        out_shape=[jax.ShapeDtypeStruct((ZS, 16, LANES), F32)] * YS,
        compiler_params=pltpu.CompilerParams(vmem_limit_bytes=VMEM_ALL),
        name="regroup",
    )(arrived)


def gram_sum_kernel(tiles_ref, *rest):
    in_refs, out_ref, total = rest[:YS], rest[YS], rest[YS + 1]
    ypos = lax.axis_index("y")
    total[...] = jnp.zeros_like(total)
    lane = lax.broadcasted_iota(jnp.int32, (8, LANES), 1)

    def add(z, carry):
        for e in range(YS):
            holder = z * YS + lax.rem(ypos - e + YS, YS)
            for j in range(CAP):
                tile = tiles_ref[j, holder]
                piece = in_refs[e][z, 8 * (j // 2):8 * (j // 2) + 8, :]
                keep = lane < CELLS if j % 2 == 0 else lane >= CELLS
                total[tile] = total[tile] + jnp.where(keep, piece, 0.0)
        return carry

    lax.fori_loop(0, ZS, add, 0)
    groups = N // TX // 2
    for b in range(ROWS // TY):
        for m in range(groups):
            first = total[2 * m * 3 + b]
            second = total[(2 * m + 1) * 3 + b]
            first = first + pltpu.roll(first, CELLS, 1)
            second = second + pltpu.roll(second, CELLS, 1)
            at = (b * groups + m) * 8
            out_ref[at:at + 8, :] = jnp.where(lane < CELLS, first, second)


def gram_sum(arrived, tiles):
    return pl.pallas_call(
        gram_sum_kernel,
        in_specs=[pl.BlockSpec(memory_space=pltpu.SMEM)] + [pl.BlockSpec(memory_space=pltpu.VMEM)] * YS,
        out_specs=pl.BlockSpec(memory_space=pltpu.VMEM),
        out_shape=jax.ShapeDtypeStruct((TILES // 2 * 8, LANES), F32),
        scratch_shapes=[pltpu.VMEM((TILES, 8, LANES), F32)],
        compiler_params=pltpu.CompilerParams(vmem_limit_bytes=VMEM_ALL),
        name="gram_sum",
    )(tiles, *arrived)


def forward_y_kernel(d_ref, s_ref, maps_ref, spread_hbm, high_ref, low_ref, out_hbm, spread_ref, out_ref, load_sem, sem):
    load = pltpu.make_async_copy(spread_hbm, spread_ref, load_sem)
    load.start()
    load.wait()
    stores = []
    for g in range(ROWS // 4):
        flipped = d_ref[4 * g:4 * g + 4].reshape(LANES, N).T
        wide = dot(jnp.concatenate(split(flipped), axis=1), spread_ref[...])
        for p in range(2):
            images, turned = [], []
            for r in (2 * p, 2 * p + 1):
                maps = dot(s_ref[4 * g + r], maps_ref[...])
                real_map, imag_map = maps[:, :LANES], maps[:, LANES:]
                d = wide[:, 2 * r * LANES:(2 * r + 1) * LANES]
                turned_d = wide[:, (2 * r + 1) * LANES:(2 * r + 2) * LANES]
                images.append(real_map * d + imag_map * turned_d)
                turned.append(real_map * turned_d - imag_map * d)
            done = transform(high_ref, low_ref, images, turned)
            pair = 2 * g + p
            store_outgoing(out_ref, 24 * pair, done[:, :LANES], done[:, LANES:])
            rows = pl.ds(24 * pair, 24)
            stores.append(pltpu.make_async_copy(out_ref.at[:, rows, :], out_hbm.at[:, rows, :], sem.at[pair]))
            stores[-1].start()
    for copy in stores:
        copy.wait()


def forward_y(direction, maps, sel_maps, sel_spread, table):
    vmem = pl.BlockSpec(memory_space=pltpu.VMEM)
    hbm = pl.BlockSpec(memory_space=pltpu.HBM)
    return pl.pallas_call(
        forward_y_kernel,
        in_specs=[vmem, vmem, vmem, hbm, vmem, vmem],
        out_specs=hbm,
        out_shape=pltpu.HBM((SLABS, BLOCK, LANES), F32),
        scratch_shapes=[
            pltpu.VMEM(sel_spread.shape, BF16),
            pltpu.VMEM((SLABS, BLOCK, LANES), F32),
            pltpu.SemaphoreType.DMA,
            pltpu.SemaphoreType.DMA((PAIRS,)),
        ],
        compiler_params=pltpu.CompilerParams(vmem_limit_bytes=VMEM_LIMIT),
        name="forward_y",
    )(*near(direction, maps, sel_maps), *far(sel_spread), *near(*table))


def arrived_rows(ref, index, block):
    parts = []
    for i in range(2):
        start = i * 8 + index if index < 8 else 16 + 4 * i + index - 8
        parts += [ref[pl.ds(start + 24 * p, SLABS, stride=block), :] for p in range(PAIRS)]
    return jnp.concatenate(parts, axis=0)


def middle_kernel(norm_ref, in_ref, *rest):
    g_hbm, tables_hbm = rest[:8], rest[8:12]
    out_ref, table_ref, g_ref, grid_ref, table_sem, g_sem = rest[12:]
    fh_ref, fl_ref, bh_ref, bl_ref = (table_ref.at[i] for i in range(4))
    xpos, core = lax.axis_index("x"), lax.axis_index("core")
    load_tables = [pltpu.make_async_copy(tables_hbm[i], table_ref.at[i], table_sem.at[i]) for i in range(4)]
    load_g = []
    for d in range(4):
        for k in range(2):
            c = 2 * lax.rem(xpos + 4 - d, 4) + lax.rem(core + k, 2)
            load_g.append(pltpu.make_async_copy(g_hbm[4 * k + d], g_ref.at[c], g_sem.at[4 * k + d]))
    for copy in load_tables[:2] + load_g + load_tables[2:]:
        copy.start()
    for p in range(PAIRS):
        pieces = [arrived_rows(in_ref, 2 * p + i, BLOCK) for i in range(2)]
        if p == 0:
            for copy in load_tables[:2]:
                copy.wait()
        done = transform(fh_ref, fl_ref, pieces, [None, None])
        for i in range(2):
            b = 2 * p + i
            grid_ref[b // TY, pl.ds(b % TY, N, stride=TY), :] = done[:, LANES * i:LANES * (i + 1)]
    for copy in load_g + load_tables[2:]:
        copy.wait()
    left = lax.broadcasted_iota(jnp.int32, (CELLS, LANES), 1) < CELLS
    curve = jnp.zeros((8, LANES), F32)
    groups = N // TX // 2
    for b in range(ROWS // TY):
        for m in range(groups):
            at = (b * groups + m) * 8
            packed = jnp.concatenate([g_ref[c, at:at + 8, :] for c in range(8)], axis=0)
            weights = jnp.concatenate([jnp.where(left, packed, 0.0), jnp.where(left, 0.0, packed)], axis=0)
            cells = slice(2 * m * CELLS, (2 * m + 2) * CELLS)
            tile = grid_ref[b, cells, :]
            w_high, w_low = split(weights)
            t_high, t_low = split(tile)
            applied = dot(jnp.concatenate([w_high, w_low], axis=1), jnp.concatenate([t_high, t_high], axis=0))
            applied = applied + dot(w_high, t_low)
            curve = curve + jnp.sum((tile * applied).reshape(2 * CELLS // 8, 8, LANES), axis=0)
            grid_ref[b, cells, :] = applied
    norm = jnp.broadcast_to(norm_ref[...], (8, LANES)) / (8 * LANES)
    sums = jnp.where(lax.broadcasted_iota(jnp.int32, (8, LANES), 0) == 0, jnp.sum(curve, axis=0, keepdims=True), norm)
    out_ref[:, BLOCK:, :] = jnp.broadcast_to(sums[None], (SLABS, 8, LANES))
    for p in range(PAIRS):
        pieces = [grid_ref[b // TY, pl.ds(b % TY, N, stride=TY), :] for b in (2 * p, 2 * p + 1)]
        done = transform(bh_ref, bl_ref, pieces, [None, None])
        store_outgoing(out_ref, 24 * p, done[:, :LANES], done[:, LANES:])


def middle(norm, arrived, grams, table_in, table_out):
    vmem = pl.BlockSpec(memory_space=pltpu.VMEM)
    hbm = pl.BlockSpec(memory_space=pltpu.HBM)
    return pl.pallas_call(
        middle_kernel,
        in_specs=[vmem] * 2 + [hbm] * 12,
        out_specs=vmem,
        out_shape=near_out(SLABS, BLOCK + 8, LANES),
        scratch_shapes=[
            pltpu.VMEM((4, N, 2 * N), BF16),
            pltpu.VMEM((8, TILES // 2 * 8, LANES), F32),
            pltpu.VMEM((ROWS // TY, N * TY, LANES), F32),
            pltpu.SemaphoreType.DMA((4,)),
            pltpu.SemaphoreType.DMA((8,)),
        ],
        compiler_params=pltpu.CompilerParams(vmem_limit_bytes=VMEM_LIMIT),
        name="middle",
    )(norm, *near(arrived), *far(*grams, *table_in, *table_out))


def backward_y_kernel(in_ref, s_ref, maps_ref, gather_ref, high_ref, low_ref, *rest):
    kept_refs, sent_refs = rest[:2], rest[2:]
    core = lax.axis_index("core")
    block = BLOCK + 8
    curve = jnp.sum(in_ref[pl.ds(BLOCK, SLABS, stride=block), :], axis=0, keepdims=True)
    norm = jnp.sum(in_ref[pl.ds(BLOCK + 1, SLABS, stride=block), :], axis=0, keepdims=True)
    sums = jnp.where(lax.broadcasted_iota(jnp.int32, (8, LANES), 0) == 0, curve, norm)
    sums = jnp.concatenate([sums] + [jnp.zeros_like(sums)] * (N // LANES - 1), axis=1)
    kept_refs[0][QUARTER:, :] = sums
    sent_refs[0][QUARTER:, :] = sums
    for g in range(ROWS // 4):
        highs, lows = [], []
        for p in range(2):
            rows = [4 * g + 2 * p + i for i in range(2)]
            pieces = [arrived_rows(in_ref, r, block) for r in rows]
            done = transform(high_ref, low_ref, pieces, [None, None])
            for i in range(2):
                back = done[:, LANES * i:LANES * (i + 1)]
                maps = dot(s_ref[rows[i]], maps_ref[...])
                high, low = split(maps[:, :LANES] * back - maps[:, LANES:] * times_i(back))
                highs.append(high)
                lows.append(low)
        total = dot(jnp.concatenate(highs + lows, axis=1), gather_ref[...]).T
        for r in range(4):
            a = 4 * g + r
            at = a % (PAIRS // 2) * 2 * PLANES
            quarter = a // (PAIRS // 2) % 2
            rows = total[2 * PLANES * r:2 * PLANES * (r + 1), :]

            @pl.when(core == a // PAIRS)
            def _():
                kept_refs[quarter][at:at + 2 * PLANES, :] = rows

            @pl.when(core != a // PAIRS)
            def _():
                sent_refs[quarter][at:at + 2 * PLANES, :] = rows


def backward_y(arrived, maps, sel_maps, sel_gather, table):
    vmem = pl.BlockSpec(memory_space=pltpu.VMEM)
    quarters = [near_out(QUARTER + 8, N), near_out(QUARTER, N)]
    return pl.pallas_call(
        backward_y_kernel,
        in_specs=[vmem] * 6,
        out_specs=[vmem] * 4,
        out_shape=quarters * 2,
        compiler_params=pltpu.CompilerParams(vmem_limit_bytes=VMEM_LIMIT),
        name="backward_y",
    )(*near(arrived, maps, sel_maps, sel_gather, *table))


def gram_kernel(counts_ref, w_ref, out_ref):
    step = pl.program_id(0)
    owners = w_ref.shape[0]
    at = pl.multiple_of((lax.axis_index("x") * 2 + lax.axis_index("core")) * 8, 8)
    lane = lax.broadcasted_iota(jnp.int32, (8, SB), 1)
    for o in range(owners):
        rows = []
        for j in range(CAP):
            live = counts_ref[j, step * owners + o]
            rows.append(jnp.where(lane < live, w_ref[o, j, pl.ds(at, 8), :], 0.0))
        l_high, l_low = split(jnp.concatenate(rows, axis=0))
        r_high, r_low = split(w_ref[o].reshape(CAP * CELLS, SB))
        both = dot_nt(jnp.concatenate([l_high, l_low], axis=0), r_high)
        gram = both[:CAP * 8] + (both[CAP * 8:] + dot_nt(l_high, r_low))
        for m in range(CAP // 2):
            first = gram[16 * m:16 * m + 8, LANES * m:LANES * (m + 1)]
            second = gram[16 * m + 8:16 * m + 16, LANES * m:LANES * (m + 1)]
            out_ref[o, 8 * m:8 * m + 8, :] = jnp.where(lane < CELLS, first, second)


def gram_rows(interp, counts):
    owners = 16
    return pl.pallas_call(
        gram_kernel,
        grid=(SLABS // owners,),
        in_specs=[pl.BlockSpec(memory_space=pltpu.SMEM), pl.BlockSpec((owners, CAP, CELLS, SB), lambda i: (i, 0, 0, 0))],
        out_specs=pl.BlockSpec((owners, 16, LANES), lambda i: (i, 0, 0)),
        out_shape=jax.ShapeDtypeStruct((SLABS, 16, LANES), F32),
        compiler_params=pltpu.CompilerParams(vmem_limit_bytes=VMEM_LIMIT),
        name="gram_rows",
    )(*far(counts, interp))


def share_kernel(a_ref, more_a_ref, b_ref, more_b_ref, residual_ref, out_ref, part_ref, sums_ref):
    first = a_ref[...] + more_a_ref[...]
    curvature = jnp.sum(first[QUARTER:QUARTER + 1, :LANES], axis=1, keepdims=True)
    norm_now = jnp.sum(first[QUARTER + 1:QUARTER + 2, :LANES], axis=1, keepdims=True)
    step = norm_now / curvature
    core = lax.axis_index("core")
    square = jnp.zeros((8, N), F32)
    for i, applied in enumerate((first[:QUARTER], b_ref[...] + more_b_ref[...])):
        rows = pl.ds(i * QUARTER, QUARTER)
        part = residual_ref[core, rows, :] - step * applied
        out_ref[rows, :] = part
        square = square + jnp.sum((part * part).reshape(QUARTER // 8, 8, N), axis=0)
    part = jnp.sum(square[:, :LANES] + square[:, LANES:2 * LANES] + square[:, 2 * LANES:], axis=0, keepdims=True)
    part_ref[...] = jnp.broadcast_to(part[None], part_ref.shape)
    sums_ref[...] = jnp.where(lax.broadcasted_iota(jnp.int32, (8, LANES), 0) == 0, step, norm_now)


def residual_share(first, second, residual):
    vmem = pl.BlockSpec(memory_space=pltpu.VMEM)
    return pl.pallas_call(
        share_kernel,
        in_specs=[vmem] * 5,
        out_specs=[vmem] * 3,
        out_shape=[
            near_out(HALF_ROWS, N),
            near_out(2 * SLABS, 1, LANES),
            near_out(8, LANES),
        ],
        compiler_params=pltpu.CompilerParams(vmem_limit_bytes=VMEM_LIMIT),
        name="residual_share",
    )(*near(*first, *second, residual))


def image_kernel(sums_ref, image_ref, direction_ref, out_ref):
    out_ref[...] = image_ref[...] + sums_ref[0:1, 0:1] * direction_ref[...]


def image_update(sums, image, direction):
    vmem = pl.BlockSpec(memory_space=pltpu.VMEM)
    return pl.pallas_call(
        image_kernel,
        in_specs=[vmem] * 3,
        out_specs=vmem,
        out_shape=jax.ShapeDtypeStruct(image.shape, F32),
        name="image_update",
    )(*near(sums, image, direction))


def finish_kernel(sums_ref, parts_ref, direction_ref, own_ref, other_ref, residual_ref, next_ref):
    ratio = jnp.sum(jnp.sum(parts_ref[...], axis=0), axis=1, keepdims=True) / sums_ref[1:2, 0:1]
    core = lax.axis_index("core")
    for half, ref in ((core, own_ref), (1 - core, other_ref)):
        residual_ref[half] = ref[...]
        next_ref[half] = ref[...] + ratio * direction_ref[half]


def finish(sums, parts, direction, own, other):
    vmem = pl.BlockSpec(memory_space=pltpu.VMEM)
    full = jax.ShapeDtypeStruct(direction.shape, F32)
    return pl.pallas_call(
        finish_kernel,
        in_specs=[vmem] * 5,
        out_specs=[vmem, vmem],
        out_shape=[full, full],
        compiler_params=pltpu.CompilerParams(vmem_limit_bytes=VMEM_LIMIT),
        name="finish",
    )(*near(sums, parts, direction, own, other))


def swap_core(value):
    return lax.ppermute(value, "core", [(0, 1), (1, 0)])


def to_next(values, axis, count):
    return list(values[:1]) + [
        lax.ppermute(values[d], axis, [(i, (i + d) % count) for i in range(count)]) for d in range(1, count)
    ]


def swap_x(value, mask):
    return lax.ppermute(value, "x", [(i, i ^ mask) for i in range(4)])


def from_x(value):
    return [lax.ppermute(value, "x", [(i, (i + d) % 4) for i in range(4)]) for d in range(1, 4)]


def body(image_x, residual, direction, sensitivity, interp, slot_tile, counts):
    sending, arrival = ([tuple(jnp.asarray(t) for t in pair) for pair in pairs] for pairs in dft_tables())
    sel_maps, sel_spread, sel_gather = (jnp.asarray(t) for t in selections())
    image_t, residual_t, direction_t = (jnp.transpose(a, (0, 2, 1)) for a in (image_x, residual, direction))

    grams = gram_rows(interp[0], counts[0].T)
    grams = lax.all_to_all(grams.reshape(ZS, YS, 16, LANES), "z", split_axis=0, concat_axis=0, tiled=True)
    outgoing = forward_y(direction_t, sensitivity, sel_maps, sel_spread, sending[0])
    outgoing, grams = lax.optimization_barrier((outgoing, grams))
    grams = regroup(grams)
    grams = gram_sum(to_next(grams, "y", YS), slot_tile[0].T)
    grams = [grams] + from_x(grams)
    grams = grams + [swap_core(g) for g in grams]

    pencils = lax.all_to_all(outgoing, SLAB, split_axis=0, concat_axis=0, tiled=True)
    norm = jnp.sum(residual_t * residual_t).reshape(1, 1)
    outgoing = middle(norm, pencils.reshape(-1, LANES), grams, arrival[0], sending[1])
    slab_rows = lax.all_to_all(outgoing, SLAB, split_axis=0, concat_axis=0, tiled=True)
    kept_a, kept_b, sent_a, sent_b = backward_y(
        slab_rows.reshape(-1, LANES), sensitivity, sel_maps, sel_gather, arrival[1]
    )

    kept_a = kept_a + swap_core(sent_a)
    kept_b = kept_b + swap_core(sent_b)
    kept_a = kept_a + swap_x(kept_a, 1)
    kept_b = kept_b + swap_x(kept_b, 3)
    halves = (2, HALF_ROWS, N)
    half, parts, sums = residual_share(
        (kept_a, swap_x(kept_a, 3)), (kept_b, swap_x(kept_b, 1)), residual_t.reshape(halves)
    )
    parts = lax.all_to_all(parts, SLAB + ("core",), split_axis=0, concat_axis=0, tiled=True)
    next_image = image_update(sums, image_t.reshape(halves), direction_t.reshape(halves))
    next_residual, next_direction = finish(sums, parts, direction_t.reshape(halves), half, swap_core(half))
    return tuple(
        jnp.transpose(a.reshape(direction_t.shape), (0, 2, 1)) for a in (next_image, next_residual, next_direction)
    )


def solution(mesh):
    fine = Mesh(mesh.devices.reshape(8, 4, 4, 2), ALL)
    rows = P(SLAB, None, None)
    return jax.shard_map(
        body,
        mesh=fine,
        in_specs=(
            rows,
            rows,
            rows,
            P(SLAB, None, COIL),
            P(SLAB, None, None, None, None),
            rows,
            rows,
        ),
        out_specs=(rows, rows, rows),
        check_vma=False,
    )
```
